128 devices in a mesh: comp: 4 (over y_lo, core), tile: 32 (over x, z, y_hi).
Axes of the slice: x: 4, y: 4 (y_hi: 2, y_lo: 2; y = y_hi * 2 + y_lo), z: 4, core: 2. Of those that a mesh axis runs over, the one named last changes fastest.
Arguments:
- state: float32 [2, 8, 256, 16384], P(None, None, 'comp', 'tile'), may hold values from -6 to 6
- courant: float32 [8, 256], P(None, 'comp'), may hold values from -0.9 to 0.9
- mixing: float32 [7, 256], P(None, 'comp'), may hold values from 0.05 to 0.24
- exchange_coef: float32 [256, 16384], P('comp', 'tile'), may hold values from 0.2 to 0.8
- sea_mask: int32 [256, 16384], P('comp', 'tile'), may hold values 0 or 1
- margin_count: int32 [4, 32, 3, 4], P('comp', 'tile'), may hold values from 0 to 4096, as said below
- margin_row: int32 [4, 32, 3, 4, 4096], P('comp', 'tile'), may hold values from 0 to 63
- margin_col: int32 [4, 32, 3, 4, 4096], P('comp', 'tile'), may hold values from 0 to 511, as said below
- margin_weight: float32 [4, 32, 3, 4, 4096], P('comp', 'tile'), may hold values from 0.05 to 0.6
Outputs:
- new_state: float32 [2, 8, 256, 16384], P(None, None, 'comp', 'tile')
- partner_surface: float32 [2, 256, 16384], P(None, 'comp', 'tile')
The draws below stay inside these ranges and needn't reach their ends.
Inputs may be any that keep to these rules, and one draw needn't show every extreme that they name: margin_count[g, t, o, h] equals margin_count[h, (t + o - 1) mod 32, 2 - o, g], and row r of the one list is the same margin as row r of the other. Only pairs of one atmosphere device (comp index below 3) and one ocean device have rows: an atmosphere device couples with the three ocean devices at tile offsets -1, 0 and 1, an ocean device with the atmosphere devices at those offsets; every such pair has at least 3584 rows. `margin_col`: for list index o = 0 (partner to the west) the columns lie below 128, for o = 2 (partner to the east) at 384 or above.
All inputs are finite; a program needn't handle non-finite values. No bound on the sum of `sea_mask` on one device may be relied on, other than what follows from the above.
Results may differ from the reference program's by a relative error of at most 0.0003.
Values sent between devices are 32-bit elements; how exact they have to be, the bound alone decides.
No kernel may reach another device: no remote copies, remote signals or barrier semaphores. Data moves between devices by JAX's collectives and lax.ppermute only.
A program may use at most 64 MiB of HBM per device.

```python
import math
import jax
import jax.numpy as jnp
from jax import lax

NF = 2
LEV = 8
SUBSTEPS = 2
BY = 64
BX = 512
CAP = 4096
ROWS = 256
COLS = 16384
N_COMP = 4
N_TILE = 32


def draw_margin_count(key, part):
    deficit = jax.random.randint(key, (N_COMP - 1, N_TILE, 3), 0, max(CAP // 8, 2))
    base = (CAP - deficit).astype(jnp.int32)
    base = base.at[0, 0, 0].set(CAP)
    full = jnp.zeros((N_COMP, N_TILE, 3, N_COMP), jnp.int32)
    full = full.at[:N_COMP - 1, :, :, N_COMP - 1].set(base)
    tiles = jnp.arange(N_TILE, dtype=jnp.int32)
    for which in range(3):
        source_tile = (tiles + which - 1) % N_TILE
        mirrored = jnp.transpose(base[:, source_tile, 2 - which], (1, 0))
        full = full.at[N_COMP - 1, :, which, :N_COMP - 1].set(mirrored)
    return full


def draw_margin_col(key, part):
    shape = (N_COMP, N_TILE, 3, N_COMP, CAP)
    anywhere = jax.random.randint(key, shape, 0, BX)
    edge = jax.random.randint(jax.random.fold_in(key, 1), shape, 0, BX // 4)
    which = jnp.arange(3, dtype=jnp.int32)[None, None, :, None, None]
    column = jnp.where(which == 0, edge, jnp.where(which == 2, BX - 1 - edge, anywhere))
    column = column.at[0, 0, 1, 0, 0].set(BX - 1)
    column = column.at[0, 0, 1, 0, 1].set(0)
    return column.astype(jnp.int32)


def with_ends(values, key, smallest, high):
    dims = values.shape
    spot = [jax.random.randint(jax.random.fold_in(key, axis), (), 0, dims[axis]) for axis in range(len(dims))]
    values = values.at[tuple(spot)].set(smallest)
    longest = dims.index(max(dims))
    spot[longest] = (spot[longest] + 1) % dims[longest]
    return values.at[tuple(spot)].set(high)


def shard_levels(rng, shape, pieces, least, high):
    def one(position, shards_of):
        heights = jax.random.uniform(jax.random.fold_in(jax.random.fold_in(rng, 6), position), (shards_of,), jnp.float32, least / len(pieces), high / len(pieces))
        return jnp.repeat(jnp.exp(heights), shape[position] // shards_of).reshape((-1,) + (1,) * (len(shape) - position - 1))

    gain = one(*pieces[0])
    for cut in pieces[1:]:
        gain = gain * one(*cut)
    return gain


def noise(stream_key, dims, width, limit, pieces=(), held_as=jnp.bfloat16):
    entries = jax.random.normal(stream_key, dims, jnp.float32) * width
    if len(pieces) > 0:
        entries = shard_levels(stream_key, dims, pieces, -0.22, 0.18) * entries
    return jnp.clip(entries, min=-limit, max=limit).astype(held_as)


def setup_inputs(seed: int = 0) -> dict:
    key_list = jax.random.split(jax.random.key(seed), 10)
    return {
        "state": noise(key_list[0], (NF, LEV, ROWS, COLS), 1.0, 6.0, ((2, 4), (3, 32)), jnp.float32),
        "courant": jnp.clip(jax.random.uniform(key_list[1], (LEV, ROWS), jnp.float32, -0.9, 0.9) * shard_levels(key_list[1], (LEV, ROWS), ((1, 4),), -0.4, 0.0), -0.9, 0.9),
        "mixing": jnp.clip(jnp.exp(math.log(0.24) - 1.5686159 * jax.random.uniform(key_list[2], (LEV - 1, ROWS), jnp.float32) ** shard_levels(key_list[2], (LEV - 1, ROWS), ((1, 4),), -0.2, 0.2)), 0.05, 0.24),
        "exchange_coef": jnp.clip(jnp.exp(math.log(0.8) - 1.3862944 * jax.random.uniform(key_list[3], (ROWS, COLS), jnp.float32) ** shard_levels(key_list[3], (ROWS, COLS), ((0, 4), (1, 32)), -0.2, 0.2)), 0.2, 0.8),
        "sea_mask": with_ends((jax.random.randint(key_list[4], (ROWS, COLS), 0, 4) < 3).astype(jnp.int32), jax.random.fold_in(key_list[4], 1), 0, 1),
        "margin_count": draw_margin_count(jax.random.fold_in(key_list[9], 71), 0),
        "margin_row": with_ends(jax.random.randint(key_list[6], (N_COMP, N_TILE, 3, N_COMP, CAP), 0, BY), jax.random.fold_in(key_list[6], 1), 0, BY - 1).astype(jnp.int32),
        "margin_col": draw_margin_col(jax.random.fold_in(key_list[9], 71), 0),
        "margin_weight": jnp.clip(0.05 + 0.55 * jax.random.uniform(key_list[8], (N_COMP, N_TILE, 3, N_COMP, CAP), jnp.float32) ** shard_levels(key_list[8], (N_COMP, N_TILE, 3, N_COMP, CAP), ((0, 4), (1, 32)), -0.2, 0.2), 0.05, 0.6),
    }


def transport(padded, speed):
    left = padded[..., :-2]
    middle = padded[..., 1:-1]
    right = padded[..., 2:]
    return middle - 0.5 * speed * (right - left) + 0.5 * speed * speed * (right - 2.0 * middle + left)


def vertical_mix(field, coeff):
    jump_up = field[:, 1:] - field[:, :-1]
    flux = coeff[None, :, :, None] * jump_up
    empty = jnp.zeros_like(flux[:, :1])
    upper = jnp.concatenate([flux, empty], axis=1)
    lower = jnp.concatenate([empty, flux], axis=1)
    return field + upper - lower


def reference(state, courant, mixing, exchange_coef, sea_mask, margin_count, margin_row, margin_col, margin_weight):
    devices_all = N_COMP * N_TILE
    cell_count = BY * BX
    surface = state[:, 0].reshape(NF, N_COMP, BY, N_TILE, BX).transpose(1, 3, 0, 2, 4).reshape(N_COMP, N_TILE, NF, cell_count)
    cells_table = (margin_row * BX + margin_col).astype(jnp.int32)
    slots = jnp.arange(CAP, dtype=jnp.int32)
    offsets = jnp.arange(3, dtype=jnp.int32)
    comp_index = jnp.arange(N_COMP, dtype=jnp.int32)[:, None]
    back_index = (2 - offsets)[None, :]

    def receive(index):
        home_comp = index // N_TILE
        home_tile = index % N_TILE
        source_tile = ((home_tile + offsets - 1) % N_TILE)[None, :]
        source_cells = cells_table[comp_index, source_tile, back_index, home_comp]
        source_counts = margin_count[comp_index, source_tile, back_index, home_comp]
        source_surface = surface[comp_index, source_tile]
        values = jnp.take_along_axis(source_surface, source_cells[:, :, None, :], axis=3)
        live = slots[None, None, :] < source_counts[:, :, None]
        values = jnp.where(live[:, :, None, :], values, 0.0)
        weights = jnp.transpose(margin_weight[home_comp, home_tile], (1, 0, 2))
        terms = values * weights[:, :, None, :]
        landing = jnp.transpose(cells_table[home_comp, home_tile], (1, 0, 2)).reshape(-1)
        flat_terms = jnp.transpose(terms, (2, 0, 1, 3)).reshape(NF, -1)
        summed = jnp.zeros((NF, cell_count), jnp.float32)
        return summed.at[:, landing].add(flat_terms)

    received = lax.map(receive, jnp.arange(devices_all, dtype=jnp.int32))
    partner = received.reshape(N_COMP, N_TILE, NF, BY, BX).transpose(2, 0, 3, 1, 4).reshape(NF, N_COMP * BY, N_TILE * BX)

    speed = courant[:, :, None]
    field = state
    for step in range(SUBSTEPS):
        padded = jnp.concatenate([field[..., -1:], field, field[..., :1]], axis=3)
        field = vertical_mix(transport(padded, speed), mixing)

    ocean = (jnp.arange(N_COMP * BY, dtype=jnp.int32) >= (N_COMP - 1) * BY)[:, None]
    rate = exchange_coef * sea_mask.astype(jnp.float32)
    first_own = field[0, 0]
    second_own = field[1, 0]
    first_far = partner[0]
    second_far = partner[1]
    new_first = first_own + rate * (first_far - first_own)
    air_second = second_own + rate * (1.2 * first_far - 0.3 * second_far - second_own)
    sea_second = second_own + rate * (1.2 * first_own - second_far)
    new_second = jnp.where(ocean, sea_second, air_second)
    field = field.at[:, 0].set(jnp.stack([new_first, new_second]))
    return field, partner
```

```python
import functools
import jax
import jax.numpy as jnp
from jax import lax
from jax.experimental import pallas as pl
from jax.experimental.pallas import tpu as pltpu
from jax.sharding import PartitionSpec as P

SUBSTEPS = 2
LANES = 128
PARTS = 4
VMEM_LIMIT = 56 * 1024 * 1024


def split_halves(values):
    high = values.astype(jnp.bfloat16)
    low = (values - high.astype(jnp.float32)).astype(jnp.bfloat16)
    return high, low


def one_hot(index_row, size):
    n = index_row.shape[1]
    inside = (index_row >= 0) & (index_row < size)
    number = jnp.where(inside, index_row, -1).astype(jnp.float32)
    number = jnp.broadcast_to(number, (16, n)).astype(jnp.bfloat16)
    blocks = []
    iota = lax.broadcasted_iota(jnp.int32, (16, n), 0).astype(jnp.float32)
    for block in range(size // 16):
        here = (iota + float(16 * block)).astype(jnp.bfloat16)
        blocks.append(jnp.where(number == here, jnp.bfloat16(1), jnp.bfloat16(0)))
    return jnp.concatenate(blocks, axis=0)


def pick(surface, columns, rows):
    width = surface.shape[1]
    total = None
    for start in range(0, width, 256):
        size = min(256, width - start)
        part = jnp.dot(
            surface[:, start : start + size],
            one_hot(columns - start, size),
            preferred_element_type=jnp.float32,
        )
        total = part if total is None else total + part
    half = total.shape[0] // 2
    total = total[:half] + total[half:]
    row_count = half // 2
    n = rows.shape[1]
    match = lax.broadcasted_iota(jnp.int32, (row_count, n), 0) == rows
    first = jnp.sum(jnp.where(match, total[:row_count], 0.0), axis=0, keepdims=True)
    second = jnp.sum(jnp.where(match, total[row_count:], 0.0), axis=0, keepdims=True)
    return first, second


def each_list(comp, ocean_comp, body):
    ocean = comp == ocean_comp
    for j in range(ocean_comp):

        @pl.when(ocean | (comp == j))
        def _():
            body(j, jnp.where(ocean, j, ocean_comp))


def edge_kernel(ocean_comp, comp_ref, row_ref, col_ref, west_ref, east_ref, to_west, to_east):
    comp = comp_ref[0]
    levels = west_ref.shape[1]
    row_count = west_ref.shape[2]
    slots = row_ref.shape[-1]
    part = slots // PARTS
    lane = lax.broadcasted_iota(jnp.int32, (row_count, LANES), 1)
    for ref, out, shift in ((west_ref, to_west, 0), (east_ref, to_east, 2)):
        tile = jnp.zeros((row_count, LANES), jnp.float32)
        for k in range(2 * levels):
            moved = pltpu.roll(ref[k // levels, k % levels], (2 * k + shift) % LANES, 1)
            tile = jnp.where(lane // 2 == k, moved, tile)
        for block in range(row_count // 8):
            start = ocean_comp * part + LANES * block
            out[:, start : start + LANES] = tile[8 * block : 8 * block + 8]
    for ref, out, o, base in (
        (west_ref, to_west, 0, 0),
        (east_ref, to_east, 2, None),
    ):
        high, low = split_halves(ref[:, 0].reshape(2 * row_count, LANES))
        surface = jnp.concatenate([high, low], axis=0)
        offset = 0 if base == 0 else EAST_OFFSET

        def one_list(j, h):
            def step(q, carry):
                span = pl.ds(pl.multiple_of(q * part, LANES), part)
                columns = col_ref[0, 0, o, pl.ds(h, 1), span] - offset
                rows = row_ref[0, 0, o, pl.ds(h, 1), span]
                first, second = pick(surface, columns, rows)
                out[pl.ds(q, 1), j * part : (j + 1) * part] = first
                out[pl.ds(q + PARTS, 1), j * part : (j + 1) * part] = second
                return carry

            lax.fori_loop(0, PARTS, step, 0)

        each_list(comp, ocean_comp, one_list)


EAST_OFFSET = 384


def centre_kernel(ocean_comp, comp_ref, row_ref, col_ref, state_ref, from_west, from_east, *outs):
    comp = comp_ref[0]
    row_count, col_count = state_ref.shape[2:]
    slots = row_ref.shape[-1]
    part = slots // PARTS
    high, low = split_halves(state_ref[:, 0].reshape(2 * row_count, col_count))
    surface = jnp.concatenate([high, low], axis=0)

    def one_list(j, h):
        out = outs[j]
        out[0] = from_west[:, j * part : (j + 1) * part]
        out[2] = from_east[:, j * part : (j + 1) * part]

        def step(q, carry):
            span = pl.ds(pl.multiple_of(q * part, LANES), part)
            columns = col_ref[0, 0, 1, pl.ds(h, 1), span]
            rows = row_ref[0, 0, 1, pl.ds(h, 1), span]
            first, second = pick(surface, columns, rows)
            out[1, pl.ds(q, 1)] = first
            out[1, pl.ds(q + PARTS, 1)] = second
            return carry

        lax.fori_loop(0, PARTS, step, 0)

    each_list(comp, ocean_comp, one_list)


def transport_kernel(halo_start, state_ref, courant_ref, mixing_ref, west_ref, east_ref, unused_ref, out_ref):
    fields, levels, rows, cols = state_ref.shape
    step = pl.program_id(0)
    full = cols + LANES
    lane = lax.broadcasted_iota(jnp.int32, (8, LANES), 1)
    for block in range(rows // 8):
        span = slice(8 * block, 8 * block + 8)
        start = pl.multiple_of(halo_start + (step * (rows // 8) + block) * LANES, LANES)
        west = west_ref[:, pl.ds(start, LANES)]
        east = east_ref[:, pl.ds(start, LANES)]
        for f in range(fields):
            field = []
            for level in range(levels):
                k = f * levels + level
                left = pltpu.roll(west, (LANES - 2 - 2 * k) % LANES, 1)
                right = pltpu.roll(east, (LANES - 2 * k) % LANES, 1)
                edge = jnp.where(lane < 64, right, left)
                field.append(jnp.concatenate([state_ref[f, level, span], edge], axis=1))
            for substep in range(SUBSTEPS):
                moved = []
                for level in range(levels):
                    q = field[level]
                    c = courant_ref[span, level : level + 1]
                    left = pltpu.roll(q, 1, 1)
                    right = pltpu.roll(q, full - 1, 1)
                    half = 0.5 * c
                    square = half * c
                    moved.append(q * (1.0 - 2.0 * square) + right * (square - half) + left * (square + half))
                flux = [
                    mixing_ref[span, level : level + 1] * (moved[level + 1] - moved[level])
                    for level in range(levels - 1)
                ]
                field = []
                for level in range(levels):
                    q = moved[level]
                    if level < levels - 1:
                        q = q + flux[level]
                    if level > 0:
                        q = q - flux[level - 1]
                    field.append(q)
            for level in range(levels):
                out_ref[f, level, span] = field[level][:, :cols]


def land_kernel(
    ocean_comp,
    comp_ref,
    count_ref,
    row_ref,
    col_ref,
    weight_ref,
    got_0,
    got_1,
    got_2,
    field_ref,
    coef_ref,
    mask_ref,
    state_out,
    partner_out,
    total_ref,
):
    comp = comp_ref[0]
    row_count, col_count = coef_ref.shape
    slots = row_ref.shape[-1]
    part = slots // PARTS
    got = (got_0, got_1, got_2)
    total_ref[...] = jnp.zeros_like(total_ref)
    slot_iota = lax.broadcasted_iota(jnp.int32, (1, part), 1)

    def one_list(j, h):
        for o, base, width in ((0, 0, LANES), (1, 0, col_count), (2, EAST_OFFSET, LANES)):
            count = count_ref[0, 0, o, h]

            def step(q, carry):
                span = pl.ds(pl.multiple_of(q * part, LANES), part)
                columns = col_ref[0, 0, o, pl.ds(h, 1), span]
                rows = row_ref[0, 0, o, pl.ds(h, 1), span]
                weights = weight_ref[0, 0, o, pl.ds(h, 1), span]
                live = slot_iota + q * part < count
                row_table = one_hot(rows, row_count) > 0
                pieces = []
                for f in range(2):
                    value = got[j][o, pl.ds(q + f * PARTS, 1)]
                    pieces.append(split_halves(jnp.where(live, weights * value, 0.0)))
                left = jnp.concatenate(
                    [
                        jnp.where(row_table, jnp.broadcast_to(pieces[f][s], row_table.shape), jnp.bfloat16(0))
                        for s in range(2)
                        for f in range(2)
                    ],
                    axis=0,
                )
                for start in range(0, width, 256):
                    size = min(256, width - start)
                    table = one_hot(columns - (base + start), size)
                    total_ref[:, base + start : base + start + size] += lax.dot_general(
                        left, table, (((1,), (1,)), ((), ())), preferred_element_type=jnp.float32
                    )
                return carry

            lax.fori_loop(0, PARTS, step, 0)

    each_list(comp, ocean_comp, one_list)
    first_far = total_ref[:row_count] + total_ref[2 * row_count : 3 * row_count]
    second_far = total_ref[row_count : 2 * row_count] + total_ref[3 * row_count :]
    partner_out[0] = first_far
    partner_out[1] = second_far
    ocean = comp == ocean_comp
    rate = coef_ref[...] * mask_ref[...].astype(jnp.float32)
    first_own = field_ref[0, 0]
    second_own = field_ref[1, 0]
    state_out[0, 0] = first_own + rate * (first_far - first_own)
    air_second = second_own + rate * (1.2 * first_far - 0.3 * second_far - second_own)
    sea_second = second_own + rate * (1.2 * first_own - second_far)
    state_out[1, 0] = jnp.where(ocean, sea_second, air_second)


def whole(array):
    return pl.BlockSpec(array.shape, functools.partial(lambda n, *i: (0,) * n, len(array.shape)))


def shards(
    state,
    courant,
    mixing,
    exchange_coef,
    sea_mask,
    margin_count,
    margin_row,
    margin_col,
    margin_weight,
):
    fields, levels, row_count, col_count = state.shape
    slots = margin_row.shape[-1]
    ocean_comp = margin_row.shape[3] - 1
    part = slots // PARTS
    tiles = lax.axis_size("tile")
    comp = lax.axis_index("comp").astype(jnp.int32).reshape(1)
    scalar = pl.BlockSpec(memory_space=pltpu.SMEM)
    params = pltpu.CompilerParams(vmem_limit_bytes=VMEM_LIMIT)
    strip = (fields, levels, row_count, LANES)
    packet = jax.ShapeDtypeStruct((2 * PARTS, ocean_comp * part + LANES * row_count // 8), jnp.float32)
    last = col_count // LANES - 1

    to_west, to_east = pl.pallas_call(
        functools.partial(edge_kernel, ocean_comp),
        grid=(1,),
        in_specs=[
            scalar,
            whole(margin_row),
            whole(margin_col),
            pl.BlockSpec(strip, lambda i: (0, 0, 0, 0)),
            pl.BlockSpec(strip, lambda i: (0, 0, 0, last)),
        ],
        out_specs=[whole(packet)] * 2,
        out_shape=[packet] * 2,
        compiler_params=params,
        name="edge_gather",
    )(comp, margin_row, margin_col, state, state)
    forward = [(i, (i + 1) % tiles) for i in range(tiles)]
    backward = [(b, a) for a, b in forward]
    from_west = lax.ppermute(to_east, "tile", forward)
    from_east = lax.ppermute(to_west, "tile", backward)

    bundle = jax.ShapeDtypeStruct((3, 2 * PARTS, part), jnp.float32)
    bundles = pl.pallas_call(
        functools.partial(centre_kernel, ocean_comp),
        grid=(1,),
        in_specs=[
            scalar,
            whole(margin_row),
            whole(margin_col),
            pl.BlockSpec((fields, 1, row_count, col_count), lambda i: (0, 0, 0, 0)),
            whole(packet),
            whole(packet),
        ],
        out_specs=[whole(bundle)] * ocean_comp,
        out_shape=[bundle] * ocean_comp,
        compiler_params=params,
        name="centre_gather",
    )(comp, margin_row, margin_col, state, from_west, from_east)
    got = []
    for g in range(ocean_comp):
        swap = []
        for t in range(tiles):
            swap.append((g * tiles + t, ocean_comp * tiles + t))
            swap.append((ocean_comp * tiles + t, g * tiles + t))
        got.append(lax.ppermute(bundles[g], ("comp", "tile"), swap))

    chunk = 16
    moved = pl.pallas_call(
        functools.partial(transport_kernel, ocean_comp * part),
        grid=(row_count // chunk,),
        in_specs=[
            pl.BlockSpec((fields, levels, chunk, col_count), lambda i: (0, 0, i, 0)),
            pl.BlockSpec((chunk, levels), lambda i: (i, 0)),
            pl.BlockSpec((chunk, levels - 1), lambda i: (i, 0)),
            whole(packet),
            whole(packet),
            pl.BlockSpec(memory_space=pl.ANY),
        ],
        out_specs=pl.BlockSpec((fields, levels, chunk, col_count), lambda i: (0, 0, i, 0)),
        out_shape=jax.ShapeDtypeStruct(state.shape, jnp.float32),
        compiler_params=params,
        name="transport",
    )(state, courant.T, mixing.T, from_west, from_east, bundles[0])

    surface_spec = pl.BlockSpec((fields, 1, row_count, col_count), lambda i: (0, 0, 0, 0))
    partner = jax.ShapeDtypeStruct((fields, row_count, col_count), jnp.float32)
    return pl.pallas_call(
        functools.partial(land_kernel, ocean_comp),
        grid=(1,),
        in_specs=[
            scalar,
            scalar,
            whole(margin_row),
            whole(margin_col),
            whole(margin_weight),
            whole(bundle),
            whole(bundle),
            whole(bundle),
            surface_spec,
            whole(exchange_coef),
            whole(sea_mask),
        ],
        out_specs=[surface_spec, whole(partner)],
        out_shape=[jax.ShapeDtypeStruct(state.shape, jnp.float32), partner],
        scratch_shapes=[pltpu.VMEM((4 * row_count, col_count), jnp.float32)],
        input_output_aliases={8: 0},
        compiler_params=params,
        name="land",
    )(
        comp,
        margin_count,
        margin_row,
        margin_col,
        margin_weight,
        *got,
        moved,
        exchange_coef,
        sea_mask,
    )


def solution(mesh):
    in_specs = (
        P(None, None, "comp", "tile"),
        P(None, "comp"),
        P(None, "comp"),
        P("comp", "tile"),
        P("comp", "tile"),
        P("comp", "tile", None, None),
        P("comp", "tile", None, None, None),
        P("comp", "tile", None, None, None),
        P("comp", "tile", None, None, None),
    )
    out_specs = (P(None, None, "comp", "tile"), P(None, "comp", "tile"))
    return jax.shard_map(shards, mesh=mesh, in_specs=in_specs, out_specs=out_specs, check_vma=False)
```

```python
import functools
import jax
import jax.numpy as jnp
from jax import lax
from jax.experimental import pallas as pl
from jax.experimental.pallas import tpu as pltpu
from jax.sharding import PartitionSpec as P

SUBSTEPS = 2
LANES = 128
PARTS = 4
VMEM_LIMIT = 56 * 1024 * 1024


def split_halves(values):
    high = values.astype(jnp.bfloat16)
    low = (values - high.astype(jnp.float32)).astype(jnp.bfloat16)
    return high, low


def one_hot(index_row, size):
    n = index_row.shape[1]
    inside = (index_row >= 0) & (index_row < size)
    number = jnp.where(inside, index_row, -1).astype(jnp.float32)
    number = jnp.broadcast_to(number, (16, n)).astype(jnp.bfloat16)
    blocks = []
    iota = lax.broadcasted_iota(jnp.int32, (16, n), 0).astype(jnp.float32)
    for block in range(size // 16):
        here = (iota + float(16 * block)).astype(jnp.bfloat16)
        blocks.append(jnp.where(number == here, jnp.bfloat16(1), jnp.bfloat16(0)))
    return jnp.concatenate(blocks, axis=0)


def match_rows(total, rows):
    row_count = total.shape[0] // 2
    match = lax.broadcasted_iota(jnp.int32, (row_count, rows.shape[1]), 0) == rows
    first = jnp.sum(jnp.where(match, total[:row_count], 0.0), axis=0, keepdims=True)
    second = jnp.sum(jnp.where(match, total[row_count:], 0.0), axis=0, keepdims=True)
    return first, second


def wide_one_hot(columns, width):
    return jnp.concatenate(
        [one_hot(columns - start, min(256, width - start)) for start in range(0, width, 256)], axis=0
    )


def edge_kernel(ocean_comp, comp_ref, row_ref, col_ref, west_ref, east_ref, to_west, to_east):
    ocean = comp_ref[0] == ocean_comp
    levels = west_ref.shape[1]
    row_count = west_ref.shape[2]
    part = row_ref.shape[-1] // PARTS
    lane = lax.broadcasted_iota(jnp.int32, (row_count, LANES), 1)
    sides = ((west_ref, to_west, 0, 0), (east_ref, to_east, 2, EAST_OFFSET))
    for ref, out, shift, unused in sides:
        tile = jnp.zeros((row_count, LANES), jnp.float32)
        for k in range(2 * levels):
            moved = pltpu.roll(ref[k // levels, k % levels], (2 * k + shift) % LANES, 1)
            tile = jnp.where(lane // 2 == k, moved, tile)
        for block in range(row_count // 8):
            start = ocean_comp * part + LANES * block
            out[:, start : start + LANES] = tile[8 * block : 8 * block + 8]

    def lists(pairs):
        for ref, out, o, offset in sides:
            high, low = split_halves(ref[:, 0].reshape(2 * row_count, LANES))
            surface = jnp.concatenate([high, low], axis=1)
            for slot, h in pairs:
                for q in range(PARTS):
                    span = slice(q * part, (q + 1) * part)
                    table = one_hot(col_ref[0, 0, o, h : h + 1, span] - offset, LANES)
                    total = jnp.dot(
                        surface,
                        jnp.concatenate([table, table], axis=0),
                        preferred_element_type=jnp.float32,
                    )
                    first, second = match_rows(total, row_ref[0, 0, o, h : h + 1, span])
                    out[q : q + 1, slot * part : (slot + 1) * part] = first
                    out[q + PARTS : q + PARTS + 1, slot * part : (slot + 1) * part] = second

    @pl.when(ocean)
    def _():
        lists([(j, j) for j in range(ocean_comp)])

    @pl.when(jnp.logical_not(ocean))
    def _():
        lists([(0, ocean_comp)])


EAST_OFFSET = 384


def centre_kernel(ocean_comp, comp_ref, row_ref, col_ref, state_ref, out):
    ocean = comp_ref[0] == ocean_comp
    row_count, col_count = state_ref.shape[2:]
    part = row_ref.shape[-1] // PARTS

    def lists(pairs):
        high, low = split_halves(state_ref[:, 0].reshape(2 * row_count, col_count))
        surface = jnp.concatenate([high, low], axis=0)
        for slot, h in pairs:
            for q in range(PARTS):
                span = slice(q * part, (q + 1) * part)
                table = wide_one_hot(col_ref[0, 0, 1, h : h + 1, span], col_count)
                total = jnp.dot(surface, table, preferred_element_type=jnp.float32)
                half = 2 * row_count
                first, second = match_rows(total[:half] + total[half:], row_ref[0, 0, 1, h : h + 1, span])
                out[slot, q : q + 1] = first
                out[slot, q + PARTS : q + PARTS + 1] = second

    @pl.when(ocean)
    def _():
        lists([(j, j) for j in range(ocean_comp)])

    @pl.when(jnp.logical_not(ocean))
    def _():
        lists([(0, ocean_comp)])


def pack_kernel(ocean_comp, comp_ref, centre_ref, from_west, from_east, *outs):
    ocean = comp_ref[0] == ocean_comp
    part = centre_ref.shape[-1]

    def fill(slots):
        for slot, out in zip(slots, outs):
            span = slice(slot * part, (slot + 1) * part)
            out[0] = from_west[:, span]
            out[1] = centre_ref[slot]
            out[2] = from_east[:, span]

    @pl.when(ocean)
    def _():
        fill(range(ocean_comp))

    @pl.when(jnp.logical_not(ocean))
    def _():
        fill([0] * ocean_comp)


def transport_kernel(halo_start, state_ref, courant_ref, mixing_ref, west_ref, east_ref, unused_ref, out_ref):
    fields, levels, rows, cols = state_ref.shape
    step = pl.program_id(0)
    full = cols + LANES
    lane = lax.broadcasted_iota(jnp.int32, (8, LANES), 1)
    tiles = cols // LANES

    def advance(q, middle, ahead, behind):
        back = [pltpu.roll(t, 1, 1) for t in q]
        fore = [pltpu.roll(t, LANES - 1, 1) for t in q]
        done = []
        for i in range(len(q)):
            left = jnp.where(lane == 0, back[i - 1], back[i])
            right = jnp.where(lane == LANES - 1, fore[(i + 1) % len(q)], fore[i])
            done.append(q[i] * middle + right * ahead + left * behind)
        return done

    for block in range(rows // 8):
        span = slice(8 * block, 8 * block + 8)
        start = pl.multiple_of(halo_start + (step * (rows // 8) + block) * LANES, LANES)
        west = west_ref[:, pl.ds(start, LANES)]
        east = east_ref[:, pl.ds(start, LANES)]
        coeffs = []
        for level in range(levels):
            c = jnp.broadcast_to(courant_ref[span, level : level + 1], (8, LANES))
            half = 0.5 * c
            square = half * c
            coeffs.append((1.0 - 2.0 * square, square - half, square + half))
        mix = [jnp.broadcast_to(mixing_ref[span, level : level + 1], (8, LANES)) for level in range(levels - 1)]
        for f in range(fields):

            def source():
                for level in range(levels):
                    k = f * levels + level
                    left = pltpu.roll(west, (LANES - 2 - 2 * k) % LANES, 1)
                    right = pltpu.roll(east, (LANES - 2 * k) % LANES, 1)
                    edge = jnp.where(lane < 64, right, left)
                    yield [state_ref[f, level, span, LANES * i : LANES * i + LANES] for i in range(tiles)] + [edge]

            def substep(stream):
                before = None
                flux_below = None
                for level, q in enumerate(stream):
                    now = advance(q, *coeffs[level])
                    if before is not None:
                        flux = [mix[level - 1] * (n - b) for n, b in zip(now, before)]
                        mixed = [b + x for b, x in zip(before, flux)]
                        if flux_below is not None:
                            mixed = [m - x for m, x in zip(mixed, flux_below)]
                        yield mixed
                        flux_below = flux
                    before = now
                yield [b - x for b, x in zip(before, flux_below)]

            stream = source()
            for unused in range(SUBSTEPS):
                stream = substep(stream)
            for level, q in enumerate(stream):
                for i in range(tiles):
                    out_ref[f, level, span, LANES * i : LANES * i + LANES] = q[i]


def land_kernel(
    ocean_comp,
    comp_ref,
    count_ref,
    row_ref,
    col_ref,
    weight_ref,
    got_0,
    got_1,
    got_2,
    field_ref,
    coef_ref,
    mask_ref,
    state_out,
    partner_out,
    centre_ref,
    west_ref,
    east_ref,
):
    ocean = comp_ref[0] == ocean_comp
    row_count, col_count = coef_ref.shape
    part = row_ref.shape[-1] // PARTS
    half_rows = row_count // 2
    slot_iota = lax.broadcasted_iota(jnp.int32, (1, part), 1)
    nt = (((1,), (1,)), ((), ()))

    def land(lists):
        for o, total_ref in ((1, centre_ref), (0, west_ref), (2, east_ref)):
            total = None
            for h, got in lists:
                count = count_ref[o, h]
                for q in range(PARTS):
                    span = slice(q * part, (q + 1) * part)
                    columns = col_ref[0, 0, o, h : h + 1, span]
                    rows = row_ref[0, 0, o, h : h + 1, span]
                    weights = weight_ref[0, 0, o, h : h + 1, span]
                    live = slot_iota + q * part < count
                    if o == 1:
                        row_table = one_hot(rows, row_count)
                        table = wide_one_hot(columns, col_count)
                    else:
                        upper = rows >= half_rows
                        row_table = one_hot(jnp.where(upper, rows - half_rows, rows), half_rows)
                        offset = EAST_OFFSET if o == 2 else 0
                        columns = columns - offset
                        table = one_hot(jnp.where(upper, columns + LANES, columns), 2 * LANES)
                    on = row_table > 0
                    pieces = []
                    for f in range(2):
                        value = got[o, q + f * PARTS : q + f * PARTS + 1]
                        pieces.append(split_halves(jnp.where(live, weights * value, 0.0)))
                    left = jnp.concatenate(
                        [
                            jnp.where(on, jnp.broadcast_to(pieces[f][s], on.shape), jnp.bfloat16(0))
                            for s in range(2)
                            for f in range(2)
                        ],
                        axis=0,
                    )
                    product = lax.dot_general(left, table, nt, preferred_element_type=jnp.float32)
                    total = product if total is None else total + product
            size = total.shape[0] // 2
            total_ref[...] = total[:size] + total[size:]

    @pl.when(ocean)
    def _():
        land([(j, got) for j, got in enumerate((got_0, got_1, got_2))])

    @pl.when(jnp.logical_not(ocean))
    def _():
        land([(ocean_comp, got_0[...] + got_1[...] + got_2[...])])

    def far(f):
        centre = centre_ref[f * row_count : (f + 1) * row_count]
        sides = []
        for ref in (west_ref, east_ref):
            rows = ref[f * half_rows : (f + 1) * half_rows]
            sides.append(jnp.concatenate([rows[:, :LANES], rows[:, LANES:]], axis=0))
        return jnp.concatenate(
            [
                centre[:, :LANES] + sides[0],
                centre[:, LANES : col_count - LANES],
                centre[:, col_count - LANES :] + sides[1],
            ],
            axis=1,
        )

    first_far = far(0)
    second_far = far(1)
    partner_out[0] = first_far
    partner_out[1] = second_far
    rate = coef_ref[...] * mask_ref[...].astype(jnp.float32)
    first_own = field_ref[0, 0]
    second_own = field_ref[1, 0]
    state_out[0, 0] = first_own + rate * (first_far - first_own)
    air_second = second_own + rate * (1.2 * first_far - 0.3 * second_far - second_own)
    sea_second = second_own + rate * (1.2 * first_own - second_far)
    state_out[1, 0] = jnp.where(ocean, sea_second, air_second)


def whole(array):
    return pl.BlockSpec(array.shape, functools.partial(lambda n, *i: (0,) * n, len(array.shape)))


def shards(
    state,
    courant,
    mixing,
    exchange_coef,
    sea_mask,
    margin_count,
    margin_row,
    margin_col,
    margin_weight,
):
    fields, levels, row_count, col_count = state.shape
    slots = margin_row.shape[-1]
    ocean_comp = margin_row.shape[3] - 1
    part = slots // PARTS
    tiles = lax.axis_size("tile")
    comp = lax.axis_index("comp").astype(jnp.int32).reshape(1)
    scalar = pl.BlockSpec(memory_space=pltpu.SMEM)
    params = pltpu.CompilerParams(vmem_limit_bytes=VMEM_LIMIT)
    strip = (fields, levels, row_count, LANES)
    packet = jax.ShapeDtypeStruct((2 * PARTS, ocean_comp * part + LANES * row_count // 8), jnp.float32)
    last = col_count // LANES - 1

    to_west, to_east = pl.pallas_call(
        functools.partial(edge_kernel, ocean_comp),
        grid=(1,),
        in_specs=[
            scalar,
            whole(margin_row),
            whole(margin_col),
            pl.BlockSpec(strip, lambda i: (0, 0, 0, 0)),
            pl.BlockSpec(strip, lambda i: (0, 0, 0, last)),
        ],
        out_specs=[whole(packet)] * 2,
        out_shape=[packet] * 2,
        compiler_params=params,
        name="edge_gather",
    )(comp, margin_row, margin_col, state, state)
    forward = [(i, (i + 1) % tiles) for i in range(tiles)]
    backward = [(b, a) for a, b in forward]
    from_west = lax.ppermute(to_east, "tile", forward)
    from_east = lax.ppermute(to_west, "tile", backward)

    bundle = jax.ShapeDtypeStruct((3, 2 * PARTS, part), jnp.float32)
    centre = pl.pallas_call(
        functools.partial(centre_kernel, ocean_comp),
        grid=(1,),
        in_specs=[
            scalar,
            whole(margin_row),
            whole(margin_col),
            pl.BlockSpec((fields, 1, row_count, col_count), lambda i: (0, 0, 0, 0)),
        ],
        out_specs=whole(bundle),
        out_shape=bundle,
        compiler_params=params,
        name="centre_gather",
    )(comp, margin_row, margin_col, state)
    bundles = pl.pallas_call(
        functools.partial(pack_kernel, ocean_comp),
        grid=(1,),
        in_specs=[scalar, whole(bundle), whole(packet), whole(packet)],
        out_specs=[whole(bundle)] * ocean_comp,
        out_shape=[bundle] * ocean_comp,
        compiler_params=params,
        name="pack",
    )(comp, centre, from_west, from_east)
    got = []
    for g in range(ocean_comp):
        swap = []
        for t in range(tiles):
            swap.append((g * tiles + t, ocean_comp * tiles + t))
            swap.append((ocean_comp * tiles + t, g * tiles + t))
        got.append(lax.ppermute(bundles[g], ("comp", "tile"), swap))

    chunk = 16
    moved = pl.pallas_call(
        functools.partial(transport_kernel, ocean_comp * part),
        grid=(row_count // chunk,),
        in_specs=[
            pl.BlockSpec((fields, levels, chunk, col_count), lambda i: (0, 0, i, 0)),
            pl.BlockSpec((chunk, levels), lambda i: (i, 0)),
            pl.BlockSpec((chunk, levels - 1), lambda i: (i, 0)),
            whole(packet),
            whole(packet),
            pl.BlockSpec(memory_space=pl.ANY),
        ],
        out_specs=pl.BlockSpec((fields, levels, chunk, col_count), lambda i: (0, 0, i, 0)),
        out_shape=jax.ShapeDtypeStruct(state.shape, jnp.float32),
        compiler_params=params,
        name="transport",
    )(state, courant.T, mixing.T, from_west, from_east, bundles[0])

    surface_spec = pl.BlockSpec((fields, 1, row_count, col_count), lambda i: (0, 0, 0, 0))
    partner = jax.ShapeDtypeStruct((fields, row_count, col_count), jnp.float32)
    return pl.pallas_call(
        functools.partial(land_kernel, ocean_comp),
        grid=(1,),
        in_specs=[
            scalar,
            scalar,
            whole(margin_row),
            whole(margin_col),
            whole(margin_weight),
            whole(bundle),
            whole(bundle),
            whole(bundle),
            surface_spec,
            whole(exchange_coef),
            whole(sea_mask),
        ],
        out_specs=[surface_spec, whole(partner)],
        out_shape=[jax.ShapeDtypeStruct(state.shape, jnp.float32), partner],
        scratch_shapes=[
            pltpu.VMEM((2 * row_count, col_count), jnp.float32),
            pltpu.VMEM((row_count, 2 * LANES), jnp.float32),
            pltpu.VMEM((row_count, 2 * LANES), jnp.float32),
        ],
        input_output_aliases={8: 0},
        compiler_params=params,
        name="land",
    )(
        comp,
        margin_count.reshape(3, ocean_comp + 1),
        margin_row,
        margin_col,
        margin_weight,
        *got,
        moved,
        exchange_coef,
        sea_mask,
    )


def solution(mesh):
    in_specs = (
        P(None, None, "comp", "tile"),
        P(None, "comp"),
        P(None, "comp"),
        P("comp", "tile"),
        P("comp", "tile"),
        P("comp", "tile", None, None),
        P("comp", "tile", None, None, None),
        P("comp", "tile", None, None, None),
        P("comp", "tile", None, None, None),
    )
    out_specs = (P(None, None, "comp", "tile"), P(None, "comp", "tile"))
    return jax.shard_map(shards, mesh=mesh, in_specs=in_specs, out_specs=out_specs, check_vma=False)
```

```python
import functools
import jax
import jax.numpy as jnp
from jax import lax
from jax.experimental import pallas as pl
from jax.experimental.pallas import tpu as pltpu
from jax.sharding import PartitionSpec as P

SUBSTEPS = 2
LANES = 128
PARTS = 4
VMEM_LIMIT = 24 * 1024 * 1024


def split_halves(values):
    high = values.astype(jnp.bfloat16)
    low = (values - high.astype(jnp.float32)).astype(jnp.bfloat16)
    return high, low


def one_hot(index_row, size):
    n = index_row.shape[1]
    inside = (index_row >= 0) & (index_row < size)
    number = jnp.where(inside, index_row, -1).astype(jnp.float32)
    number = jnp.broadcast_to(number, (16, n)).astype(jnp.bfloat16)
    blocks = []
    iota = lax.broadcasted_iota(jnp.int32, (16, n), 0).astype(jnp.float32)
    for block in range(size // 16):
        here = (iota + float(16 * block)).astype(jnp.bfloat16)
        blocks.append(jnp.where(number == here, jnp.bfloat16(1), jnp.bfloat16(0)))
    return jnp.concatenate(blocks, axis=0)


def match_rows(total, rows):
    row_count = total.shape[0] // 2
    match = lax.broadcasted_iota(jnp.int32, (row_count, rows.shape[1]), 0) == rows
    first = jnp.sum(jnp.where(match, total[:row_count], 0.0), axis=0, keepdims=True)
    second = jnp.sum(jnp.where(match, total[row_count:], 0.0), axis=0, keepdims=True)
    return first, second


def wide_one_hot(columns, width):
    return jnp.concatenate(
        [one_hot(columns - start, min(256, width - start)) for start in range(0, width, 256)], axis=0
    )


def edge_kernel(ocean_comp, comp_ref, row_ref, col_ref, west_ref, east_ref, to_west, to_east):
    ocean = comp_ref[0] == ocean_comp
    levels = west_ref.shape[1]
    row_count = west_ref.shape[2]
    part = row_ref.shape[-1] // PARTS
    lane = lax.broadcasted_iota(jnp.int32, (row_count, LANES), 1)
    sides = ((west_ref, to_west, 0, 0), (east_ref, to_east, 2, EAST_OFFSET))
    for ref, out, shift, unused in sides:
        tile = jnp.zeros((row_count, LANES), jnp.float32)
        for k in range(2 * levels):
            moved = pltpu.roll(ref[k // levels, k % levels], (2 * k + shift) % LANES, 1)
            tile = jnp.where(lane // 2 == k, moved, tile)
        for block in range(row_count // 8):
            start = ocean_comp * part + LANES * block
            out[:, start : start + LANES] = tile[8 * block : 8 * block + 8]

    def lists(pairs):
        for ref, out, o, offset in sides:
            high, low = split_halves(ref[:, 0].reshape(2 * row_count, LANES))
            surface = jnp.concatenate([high, low], axis=1)
            for slot, h in pairs:
                for q in range(PARTS):
                    span = slice(q * part, (q + 1) * part)
                    table = one_hot(col_ref[0, 0, o, h : h + 1, span] - offset, LANES)
                    total = jnp.dot(
                        surface,
                        jnp.concatenate([table, table], axis=0),
                        preferred_element_type=jnp.float32,
                    )
                    first, second = match_rows(total, row_ref[0, 0, o, h : h + 1, span])
                    out[q : q + 1, slot * part : (slot + 1) * part] = first
                    out[q + PARTS : q + PARTS + 1, slot * part : (slot + 1) * part] = second

    @pl.when(ocean)
    def _():
        lists([(j, j) for j in range(ocean_comp)])

    @pl.when(jnp.logical_not(ocean))
    def _():
        lists([(0, ocean_comp)])


EAST_OFFSET = 384


def centre_kernel(ocean_comp, comp_ref, row_ref, col_ref, state_ref, out):
    ocean = comp_ref[0] == ocean_comp
    row_count, col_count = state_ref.shape[2:]
    part = row_ref.shape[-1] // PARTS

    def lists(pairs):
        high, low = split_halves(state_ref[:, 0].reshape(2 * row_count, col_count))
        surface = jnp.concatenate([high, low], axis=0)
        for slot, h in pairs:
            for q in range(PARTS):
                span = slice(q * part, (q + 1) * part)
                table = wide_one_hot(col_ref[0, 0, 1, h : h + 1, span], col_count)
                total = jnp.dot(surface, table, preferred_element_type=jnp.float32)
                half = 2 * row_count
                first, second = match_rows(total[:half] + total[half:], row_ref[0, 0, 1, h : h + 1, span])
                out[slot, q : q + 1] = first
                out[slot, q + PARTS : q + PARTS + 1] = second

    @pl.when(ocean)
    def _():
        lists([(j, j) for j in range(ocean_comp)])

    @pl.when(jnp.logical_not(ocean))
    def _():
        lists([(0, ocean_comp)])


def pack_kernel(ocean_comp, comp_ref, count_ref, centre_ref, from_west, from_east, *outs):
    ocean = comp_ref[0] == ocean_comp
    part = centre_ref.shape[-1]

    def fill(slots):
        for slot, out in zip(slots, outs):
            span = slice(slot * part, (slot + 1) * part)
            out[0] = from_west[:, span]
            out[1] = centre_ref[slot]
            out[2] = from_east[:, span]

    @pl.when(ocean)
    def _():
        fill(range(ocean_comp))

    @pl.when(jnp.logical_not(ocean))
    def _():
        fill([0] * ocean_comp)


def transport_kernel(
    halo_start, state_ref, courant_ref, mixing_ref, west_ref, east_ref, unused_ref, out_ref, courant_by_row, mixing_by_row
):
    fields, levels, rows, cols = state_ref.shape
    step = pl.program_id(0)
    tiles = cols // LANES

    @pl.when(step == 0)
    def _():
        courant_by_row[...] = courant_ref[...].T
        mixing_by_row[...] = mixing_ref[...].T

    def spread(ref, level):
        here = pl.ds(pl.multiple_of(step * rows, 8), rows)
        return jnp.broadcast_to(ref[here, level : level + 1], (rows, LANES))[None]

    source = lax.broadcasted_iota(jnp.int32, (2 * LANES, 2 * LANES), 0) % LANES
    target = lax.broadcasted_iota(jnp.int32, (2 * LANES, 2 * LANES), 1)
    wanted = jnp.where(target < LANES, (target + LANES - 1) % LANES, (target + 1) % LANES)
    mover = jnp.where(source == wanted, 1.0, 0.0).astype(jnp.bfloat16)
    lane = lax.broadcasted_iota(jnp.int32, (levels, rows, LANES), 2)
    low_end = lane == 0
    high_end = lane == LANES - 1
    halo_lane = lax.broadcasted_iota(jnp.int32, (8, LANES), 1)

    speed = jnp.concatenate([spread(courant_by_row, level) for level in range(levels)], axis=0)
    half = 0.5 * speed
    square = half * speed
    middle, ahead, behind = 1.0 - 2.0 * square, square - half, square + half
    mix = jnp.concatenate([spread(mixing_by_row, level) for level in range(levels - 1)], axis=0)
    for f in range(fields):
        edges = []
        for level in range(levels):
            k = f * levels + level
            blocks = []
            for block in range(rows // 8):
                start = pl.multiple_of(halo_start + (step * (rows // 8) + block) * LANES, LANES)
                left = pltpu.roll(west_ref[:, pl.ds(start, LANES)], (LANES - 2 - 2 * k) % LANES, 1)
                right = pltpu.roll(east_ref[:, pl.ds(start, LANES)], (LANES - 2 * k) % LANES, 1)
                blocks.append(jnp.where(halo_lane < LANES // 2, right, left))
            edges.append(jnp.concatenate(blocks, axis=0)[None])
        field = [state_ref[f, :, :, LANES * i : LANES * i + LANES] for i in range(tiles)]
        field.append(jnp.concatenate(edges, axis=0))
        for substep in range(SUBSTEPS):
            back, fore = [], []
            for tile in field:
                pair = jnp.concatenate(split_halves(tile.reshape(levels * rows, LANES)), axis=1)
                moved = jnp.dot(pair, mover, preferred_element_type=jnp.float32)
                back.append(moved[:, :LANES].reshape(tile.shape))
                fore.append(moved[:, LANES:].reshape(tile.shape))
            count = tiles if substep == SUBSTEPS - 1 else tiles + 1
            after = []
            for i in range(count):
                left = jnp.where(low_end, back[i - 1], back[i])
                right = jnp.where(high_end, fore[(i + 1) % (tiles + 1)], fore[i])
                q = field[i] * middle + right * ahead + left * behind
                flux = mix * (q[1:] - q[:-1])
                after.append(
                    jnp.concatenate([q[:1] + flux[:1], q[1:-1] + flux[1:] - flux[:-1], q[-1:] - flux[-1:]], axis=0)
                )
            field = after
        for i in range(tiles):
            out_ref[f, :, :, LANES * i : LANES * i + LANES] = field[i]


def land_kernel(
    ocean_comp,
    comp_ref,
    count_ref,
    row_ref,
    col_ref,
    weight_ref,
    got_0,
    got_1,
    got_2,
    field_ref,
    coef_ref,
    mask_ref,
    state_out,
    partner_out,
    centre_ref,
    west_ref,
    east_ref,
):
    ocean = comp_ref[0] == ocean_comp
    row_count, col_count = coef_ref.shape
    part = row_ref.shape[-1] // PARTS
    half_rows = row_count // 2
    slot_iota = lax.broadcasted_iota(jnp.int32, (1, part), 1)
    nt = (((1,), (1,)), ((), ()))

    def land(lists):
        for o, total_ref in ((1, centre_ref), (0, west_ref), (2, east_ref)):
            total = None
            for h, got in lists:
                count = count_ref[o, h]
                for q in range(PARTS):
                    span = slice(q * part, (q + 1) * part)
                    columns = col_ref[0, 0, o, h : h + 1, span]
                    rows = row_ref[0, 0, o, h : h + 1, span]
                    weights = weight_ref[0, 0, o, h : h + 1, span]
                    live = slot_iota + q * part < count
                    if o == 1:
                        row_table = one_hot(rows, row_count)
                        table = wide_one_hot(columns, col_count)
                    else:
                        upper = rows >= half_rows
                        row_table = one_hot(jnp.where(upper, rows - half_rows, rows), half_rows)
                        offset = EAST_OFFSET if o == 2 else 0
                        columns = columns - offset
                        table = one_hot(jnp.where(upper, columns + LANES, columns), 2 * LANES)
                    on = row_table > 0
                    pieces = []
                    for f in range(2):
                        value = got[o, q + f * PARTS : q + f * PARTS + 1]
                        pieces.append(split_halves(jnp.where(live, weights * value, 0.0)))
                    left = jnp.concatenate(
                        [
                            jnp.where(on, jnp.broadcast_to(pieces[f][s], on.shape), jnp.bfloat16(0))
                            for s in range(2)
                            for f in range(2)
                        ],
                        axis=0,
                    )
                    product = lax.dot_general(left, table, nt, preferred_element_type=jnp.float32)
                    total = product if total is None else total + product
            size = total.shape[0] // 2
            total_ref[...] = total[:size] + total[size:]

    @pl.when(ocean)
    def _():
        land([(j, got) for j, got in enumerate((got_0, got_1, got_2))])

    @pl.when(jnp.logical_not(ocean))
    def _():
        land([(ocean_comp, got_0[...] + got_1[...] + got_2[...])])

    def far(f):
        centre = centre_ref[f * row_count : (f + 1) * row_count]
        sides = []
        for ref in (west_ref, east_ref):
            rows = ref[f * half_rows : (f + 1) * half_rows]
            sides.append(jnp.concatenate([rows[:, :LANES], rows[:, LANES:]], axis=0))
        return jnp.concatenate(
            [
                centre[:, :LANES] + sides[0],
                centre[:, LANES : col_count - LANES],
                centre[:, col_count - LANES :] + sides[1],
            ],
            axis=1,
        )

    first_far = far(0)
    second_far = far(1)
    partner_out[0] = first_far
    partner_out[1] = second_far
    rate = coef_ref[...] * mask_ref[...].astype(jnp.float32)
    first_own = field_ref[0, 0]
    second_own = field_ref[1, 0]
    state_out[0, 0] = first_own + rate * (first_far - first_own)
    air_second = second_own + rate * (1.2 * first_far - 0.3 * second_far - second_own)
    sea_second = second_own + rate * (1.2 * first_own - second_far)
    state_out[1, 0] = jnp.where(ocean, sea_second, air_second)


def whole(array):
    return pl.BlockSpec(array.shape, functools.partial(lambda n, *i: (0,) * n, len(array.shape)))


def shards(
    state,
    courant,
    mixing,
    exchange_coef,
    sea_mask,
    margin_count,
    margin_row,
    margin_col,
    margin_weight,
):
    fields, levels, row_count, col_count = state.shape
    slots = margin_row.shape[-1]
    ocean_comp = margin_row.shape[3] - 1
    part = slots // PARTS
    tiles = lax.axis_size("tile")
    comp = lax.axis_index("comp").astype(jnp.int32).reshape(1)
    counts = margin_count.reshape(3, ocean_comp + 1)
    scalar = pl.BlockSpec(memory_space=pltpu.SMEM)
    params = pltpu.CompilerParams(vmem_limit_bytes=VMEM_LIMIT)
    strip = (fields, levels, row_count, LANES)
    packet = jax.ShapeDtypeStruct((2 * PARTS, ocean_comp * part + LANES * row_count // 8), jnp.float32)
    last = col_count // LANES - 1

    to_west, to_east = pl.pallas_call(
        functools.partial(edge_kernel, ocean_comp),
        grid=(1,),
        in_specs=[
            scalar,
            whole(margin_row),
            whole(margin_col),
            pl.BlockSpec(strip, lambda i: (0, 0, 0, 0)),
            pl.BlockSpec(strip, lambda i: (0, 0, 0, last)),
        ],
        out_specs=[whole(packet)] * 2,
        out_shape=[packet] * 2,
        compiler_params=params,
        name="edge_gather",
    )(comp, margin_row, margin_col, state, state)
    forward = [(i, (i + 1) % tiles) for i in range(tiles)]
    backward = [(b, a) for a, b in forward]
    from_west = lax.ppermute(to_east, "tile", forward)
    from_east = lax.ppermute(to_west, "tile", backward)

    bundle = jax.ShapeDtypeStruct((3, 2 * PARTS, part), jnp.float32)
    centre = pl.pallas_call(
        functools.partial(centre_kernel, ocean_comp),
        grid=(1,),
        in_specs=[
            scalar,
            whole(margin_row),
            whole(margin_col),
            pl.BlockSpec((fields, 1, row_count, col_count), lambda i: (0, 0, 0, 0)),
        ],
        out_specs=whole(bundle),
        out_shape=bundle,
        compiler_params=params,
        name="centre_gather",
    )(comp, margin_row, margin_col, state)
    bundles = pl.pallas_call(
        functools.partial(pack_kernel, ocean_comp),
        grid=(1,),
        in_specs=[scalar, scalar, whole(bundle), whole(packet), whole(packet)],
        out_specs=[whole(bundle)] * ocean_comp,
        out_shape=[bundle] * ocean_comp,
        compiler_params=params,
        name="pack",
    )(comp, counts, centre, from_west, from_east)
    got = []
    for g in range(ocean_comp):
        swap = []
        for t in range(tiles):
            swap.append((g * tiles + t, ocean_comp * tiles + t))
            swap.append((ocean_comp * tiles + t, g * tiles + t))
        got.append(lax.ppermute(bundles[g], ("comp", "tile"), swap))

    chunk = 32
    moved = pl.pallas_call(
        functools.partial(transport_kernel, ocean_comp * part),
        grid=(row_count // chunk,),
        in_specs=[
            pl.BlockSpec((fields, levels, chunk, col_count), lambda i: (0, 0, i, 0)),
            whole(courant),
            whole(mixing),
            whole(packet),
            whole(packet),
            pl.BlockSpec(memory_space=pl.ANY),
        ],
        out_specs=pl.BlockSpec((fields, levels, chunk, col_count), lambda i: (0, 0, i, 0)),
        out_shape=jax.ShapeDtypeStruct(state.shape, jnp.float32),
        scratch_shapes=[
            pltpu.VMEM((row_count, levels), jnp.float32),
            pltpu.VMEM((row_count, levels - 1), jnp.float32),
        ],
        compiler_params=params,
        name="transport",
    )(state, courant, mixing, from_west, from_east, bundles[0])

    surface_spec = pl.BlockSpec((fields, 1, row_count, col_count), lambda i: (0, 0, 0, 0))
    partner = jax.ShapeDtypeStruct((fields, row_count, col_count), jnp.float32)
    return pl.pallas_call(
        functools.partial(land_kernel, ocean_comp),
        grid=(1,),
        in_specs=[
            scalar,
            scalar,
            whole(margin_row),
            whole(margin_col),
            whole(margin_weight),
            whole(bundle),
            whole(bundle),
            whole(bundle),
            surface_spec,
            whole(exchange_coef),
            whole(sea_mask),
        ],
        out_specs=[surface_spec, whole(partner)],
        out_shape=[jax.ShapeDtypeStruct(state.shape, jnp.float32), partner],
        scratch_shapes=[
            pltpu.VMEM((2 * row_count, col_count), jnp.float32),
            pltpu.VMEM((row_count, 2 * LANES), jnp.float32),
            pltpu.VMEM((row_count, 2 * LANES), jnp.float32),
        ],
        input_output_aliases={8: 0},
        compiler_params=params,
        name="land",
    )(
        comp,
        counts,
        margin_row,
        margin_col,
        margin_weight,
        *got,
        moved,
        exchange_coef,
        sea_mask,
    )


def solution(mesh):
    in_specs = (
        P(None, None, "comp", "tile"),
        P(None, "comp"),
        P(None, "comp"),
        P("comp", "tile"),
        P("comp", "tile"),
        P("comp", "tile", None, None),
        P("comp", "tile", None, None, None),
        P("comp", "tile", None, None, None),
        P("comp", "tile", None, None, None),
    )
    out_specs = (P(None, None, "comp", "tile"), P(None, "comp", "tile"))
    return jax.shard_map(shards, mesh=mesh, in_specs=in_specs, out_specs=out_specs, check_vma=False)
```

```python
import functools
import jax
import jax.numpy as jnp
from jax import lax
from jax.experimental import pallas as pl
from jax.experimental.pallas import tpu as pltpu
from jax.sharding import PartitionSpec as P

SUBSTEPS = 2
LANES = 128
PARTS = 4
VMEM_LIMIT = 24 * 1024 * 1024
FIRST_VMEM_LIMIT = 60 * 1024 * 1024


def split_halves(values):
    high = values.astype(jnp.bfloat16)
    low = (values - high.astype(jnp.float32)).astype(jnp.bfloat16)
    return high, low


def one_hot(index_row, size):
    n = index_row.shape[1]
    inside = (index_row >= 0) & (index_row < size)
    number = jnp.where(inside, index_row, -1).astype(jnp.float32)
    number = jnp.broadcast_to(number, (16, n)).astype(jnp.bfloat16)
    blocks = []
    iota = lax.broadcasted_iota(jnp.int32, (16, n), 0).astype(jnp.float32)
    for block in range(size // 16):
        here = (iota + float(16 * block)).astype(jnp.bfloat16)
        blocks.append(jnp.where(number == here, jnp.bfloat16(1), jnp.bfloat16(0)))
    return jnp.concatenate(blocks, axis=0)


def match_rows(total, rows):
    row_count = total.shape[0] // 2
    match = lax.broadcasted_iota(jnp.int32, (row_count, rows.shape[1]), 0) == rows
    first = jnp.sum(jnp.where(match, total[:row_count], 0.0), axis=0, keepdims=True)
    second = jnp.sum(jnp.where(match, total[row_count:], 0.0), axis=0, keepdims=True)
    return first, second


def wide_one_hot(columns, width):
    return jnp.concatenate(
        [one_hot(columns - start, min(256, width - start)) for start in range(0, width, 256)], axis=0
    )


def edge_kernel(
    ocean_comp,
    comp_ref,
    row_hbm,
    col_hbm,
    state_hbm,
    to_west,
    to_east,
    row_ref,
    col_ref,
    west_top,
    east_top,
    west_all,
    east_all,
    sems,
):
    ocean = comp_ref[0] == ocean_comp
    levels = west_all.shape[1]
    row_count = west_all.shape[2]
    part = row_ref.shape[-1] // PARTS
    cols = state_hbm.shape[3]
    near = slice(0, LANES)
    far = slice(cols - LANES, cols)
    copies = [
        pltpu.make_async_copy(source, target, sems.at[i])
        for i, (source, target) in enumerate(
            (
                (col_hbm, col_ref),
                (row_hbm, row_ref),
                (state_hbm.at[:, 0:1, :, near], west_top),
                (state_hbm.at[:, 0:1, :, far], east_top),
                (state_hbm.at[:, :, :, near], west_all),
                (state_hbm.at[:, :, :, far], east_all),
            )
        )
    ]
    for copy in copies:
        copy.start()
    sides = ((west_top, to_west, 0, 0), (east_top, to_east, 2, EAST_OFFSET))
    for copy in copies[:4]:
        copy.wait()

    def lists(pairs):
        for ref, out, o, offset in sides:
            high, low = split_halves(ref[:, 0].reshape(2 * row_count, LANES))
            surface = jnp.concatenate([high, low], axis=1)
            for slot, h in pairs:
                for q in range(PARTS):
                    span = slice(q * part, (q + 1) * part)
                    table = one_hot(col_ref[0, 0, o, h : h + 1, span] - offset, LANES)
                    total = jnp.dot(
                        surface,
                        jnp.concatenate([table, table], axis=0),
                        preferred_element_type=jnp.float32,
                    )
                    first, second = match_rows(total, row_ref[0, 0, o, h : h + 1, span])
                    out[q : q + 1, slot * part : (slot + 1) * part] = first
                    out[q + PARTS : q + PARTS + 1, slot * part : (slot + 1) * part] = second

    @pl.when(ocean)
    def _():
        lists([(j, j) for j in range(ocean_comp)])

    @pl.when(jnp.logical_not(ocean))
    def _():
        lists([(0, ocean_comp)])

    for copy in copies[4:]:
        copy.wait()
    lane = lax.broadcasted_iota(jnp.int32, (HALO_ROWS, LANES), 1)
    for ref, out, shift in ((west_all, to_west, 0), (east_all, to_east, 2)):
        tile = jnp.zeros((HALO_ROWS, LANES), jnp.float32)
        for group in range(row_count // HALO_ROWS):
            for k in range(2 * levels):
                at = 2 * k + group * HALO_LANES
                rows = ref[k // levels, k % levels, group * HALO_ROWS : (group + 1) * HALO_ROWS]
                tile = jnp.where(lane // 2 == at // 2, pltpu.roll(rows, (at + shift) % LANES, 1), tile)
        for block in range(HALO_ROWS // 8):
            start = ocean_comp * part + LANES * block
            out[:, start : start + LANES] = tile[8 * block : 8 * block + 8]


HALO_ROWS = 16
HALO_LANES = 32
EAST_OFFSET = 384


def centre_kernel(ocean_comp, comp_ref, row_ref, col_ref, state_ref, out):
    ocean = comp_ref[0] == ocean_comp
    row_count, col_count = state_ref.shape[2:]
    part = row_ref.shape[-1] // PARTS

    def lists(pairs):
        high, low = split_halves(state_ref[:, 0].reshape(2 * row_count, col_count))
        surface = jnp.concatenate([high, low], axis=0)
        for slot, h in pairs:
            for q in range(PARTS):
                span = slice(q * part, (q + 1) * part)
                table = wide_one_hot(col_ref[0, 0, 1, h : h + 1, span], col_count)
                total = jnp.dot(surface, table, preferred_element_type=jnp.float32)
                half = 2 * row_count
                first, second = match_rows(total[:half] + total[half:], row_ref[0, 0, 1, h : h + 1, span])
                out[slot, q : q + 1] = first
                out[slot, q + PARTS : q + PARTS + 1] = second

    @pl.when(ocean)
    def _():
        lists([(j, j) for j in range(ocean_comp)])

    @pl.when(jnp.logical_not(ocean))
    def _():
        lists([(0, ocean_comp)])


def pack_kernel(ocean_comp, comp_ref, count_ref, centre_ref, from_west, from_east, *outs):
    ocean = comp_ref[0] == ocean_comp
    part = centre_ref.shape[-1]

    def fill(slots):
        for slot, out in zip(slots, outs):
            span = slice(slot * part, (slot + 1) * part)
            out[0] = from_west[:, span]
            out[1] = centre_ref[slot]
            out[2] = from_east[:, span]

    @pl.when(ocean)
    def _():
        fill(range(ocean_comp))

    @pl.when(jnp.logical_not(ocean))
    def _():
        fill([0] * ocean_comp)


def transport_kernel(
    halo_start, state_ref, courant_ref, mixing_ref, west_ref, east_ref, unused_ref, out_ref, courant_by_row, mixing_by_row
):
    fields, levels, rows, cols = state_ref.shape
    step = pl.program_id(0)
    tiles = cols // LANES

    @pl.when(step == 0)
    def _():
        courant_by_row[...] = courant_ref[...].T
        mixing_by_row[...] = mixing_ref[...].T

    def spread(ref, level):
        here = pl.ds(pl.multiple_of(step * rows, 8), rows)
        return jnp.broadcast_to(ref[here, level : level + 1], (rows, LANES))[None]

    source = lax.broadcasted_iota(jnp.int32, (2 * LANES, 2 * LANES), 0) % LANES
    target = lax.broadcasted_iota(jnp.int32, (2 * LANES, 2 * LANES), 1)
    wanted = jnp.where(target < LANES, (target + LANES - 1) % LANES, (target + 1) % LANES)
    mover = jnp.where(source == wanted, 1.0, 0.0).astype(jnp.bfloat16)
    lane = lax.broadcasted_iota(jnp.int32, (levels, rows, LANES), 2)
    low_end = lane == 0
    high_end = lane == LANES - 1
    halo_lane = lax.broadcasted_iota(jnp.int32, (8, LANES), 1)

    speed = jnp.concatenate([spread(courant_by_row, level) for level in range(levels)], axis=0)
    half = 0.5 * speed
    square = half * speed
    middle, ahead, behind = 1.0 - 2.0 * square, square - half, square + half
    mix = jnp.concatenate([spread(mixing_by_row, level) for level in range(levels - 1)], axis=0)
    for f in range(fields):
        edges = []
        for level in range(levels):
            k = f * levels + level
            blocks = []
            for block in range(rows // 8):
                inner = 8 * block % HALO_ROWS // 8
                start = halo_start + inner * LANES
                group = step * (rows // HALO_ROWS) + 8 * block // HALO_ROWS
                at = 2 * k + group * HALO_LANES
                left = pltpu.roll(west_ref[:, start : start + LANES], (2 * LANES - 2 - at) % LANES, 1)
                right = pltpu.roll(east_ref[:, start : start + LANES], (LANES - at) % LANES, 1)
                blocks.append(jnp.where(halo_lane < LANES // 2, right, left))
            edges.append(jnp.concatenate(blocks, axis=0)[None])
        field = [state_ref[f, :, :, LANES * i : LANES * i + LANES] for i in range(tiles)]
        field.append(jnp.concatenate(edges, axis=0))
        for substep in range(SUBSTEPS):
            back, fore = [], []
            for tile in field:
                pair = jnp.concatenate(split_halves(tile.reshape(levels * rows, LANES)), axis=1)
                moved = jnp.dot(pair, mover, preferred_element_type=jnp.float32)
                back.append(moved[:, :LANES].reshape(tile.shape))
                fore.append(moved[:, LANES:].reshape(tile.shape))
            count = tiles if substep == SUBSTEPS - 1 else tiles + 1
            after = []
            for i in range(count):
                left = jnp.where(low_end, back[i - 1], back[i])
                right = jnp.where(high_end, fore[(i + 1) % (tiles + 1)], fore[i])
                q = field[i] * middle + right * ahead + left * behind
                flux = mix * (q[1:] - q[:-1])
                after.append(
                    jnp.concatenate([q[:1] + flux[:1], q[1:-1] + flux[1:] - flux[:-1], q[-1:] - flux[-1:]], axis=0)
                )
            field = after
        for i in range(tiles):
            out_ref[f, :, :, LANES * i : LANES * i + LANES] = field[i]


def land_kernel(
    ocean_comp,
    comp_ref,
    count_ref,
    row_ref,
    col_ref,
    weight_ref,
    got_0,
    got_1,
    got_2,
    field_ref,
    coef_ref,
    mask_ref,
    state_out,
    partner_out,
    centre_ref,
    west_ref,
    east_ref,
):
    ocean = comp_ref[0] == ocean_comp
    row_count, col_count = coef_ref.shape
    part = row_ref.shape[-1] // PARTS
    half_rows = row_count // 2
    slot_iota = lax.broadcasted_iota(jnp.int32, (1, part), 1)
    nt = (((1,), (1,)), ((), ()))

    def land(lists):
        for o, total_ref in ((1, centre_ref), (0, west_ref), (2, east_ref)):
            total = None
            for h, got in lists:
                count = count_ref[o, h]
                for q in range(PARTS):
                    span = slice(q * part, (q + 1) * part)
                    columns = col_ref[0, 0, o, h : h + 1, span]
                    rows = row_ref[0, 0, o, h : h + 1, span]
                    weights = weight_ref[0, 0, o, h : h + 1, span]
                    live = slot_iota + q * part < count
                    if o == 1:
                        row_table = one_hot(rows, row_count)
                        table = wide_one_hot(columns, col_count)
                    else:
                        upper = rows >= half_rows
                        row_table = one_hot(jnp.where(upper, rows - half_rows, rows), half_rows)
                        offset = EAST_OFFSET if o == 2 else 0
                        columns = columns - offset
                        table = one_hot(jnp.where(upper, columns + LANES, columns), 2 * LANES)
                    on = row_table > 0
                    pieces = []
                    for f in range(2):
                        value = got[o, q + f * PARTS : q + f * PARTS + 1]
                        pieces.append(split_halves(jnp.where(live, weights * value, 0.0)))
                    left = jnp.concatenate(
                        [
                            jnp.where(on, jnp.broadcast_to(pieces[f][s], on.shape), jnp.bfloat16(0))
                            for s in range(2)
                            for f in range(2)
                        ],
                        axis=0,
                    )
                    product = lax.dot_general(left, table, nt, preferred_element_type=jnp.float32)
                    total = product if total is None else total + product
            size = total.shape[0] // 2
            total_ref[...] = total[:size] + total[size:]

    @pl.when(ocean)
    def _():
        land([(j, got) for j, got in enumerate((got_0, got_1, got_2))])

    @pl.when(jnp.logical_not(ocean))
    def _():
        comp = comp_ref[0]
        mine = jnp.where(comp == 0, got_0[...], jnp.where(comp == 1, got_1[...], got_2[...]))
        land([(ocean_comp, mine)])

    def far(f):
        centre = centre_ref[f * row_count : (f + 1) * row_count]
        sides = []
        for ref in (west_ref, east_ref):
            rows = ref[f * half_rows : (f + 1) * half_rows]
            sides.append(jnp.concatenate([rows[:, :LANES], rows[:, LANES:]], axis=0))
        return jnp.concatenate(
            [
                centre[:, :LANES] + sides[0],
                centre[:, LANES : col_count - LANES],
                centre[:, col_count - LANES :] + sides[1],
            ],
            axis=1,
        )

    first_far = far(0)
    second_far = far(1)
    partner_out[0] = first_far
    partner_out[1] = second_far
    rate = coef_ref[...] * mask_ref[...].astype(jnp.float32)
    first_own = field_ref[0, 0]
    second_own = field_ref[1, 0]
    state_out[0, 0] = first_own + rate * (first_far - first_own)
    air_second = second_own + rate * (1.2 * first_far - 0.3 * second_far - second_own)
    sea_second = second_own + rate * (1.2 * first_own - second_far)
    state_out[1, 0] = jnp.where(ocean, sea_second, air_second)


def whole(array):
    return pl.BlockSpec(array.shape, functools.partial(lambda n, *i: (0,) * n, len(array.shape)))


def shards(
    state,
    courant,
    mixing,
    exchange_coef,
    sea_mask,
    margin_count,
    margin_row,
    margin_col,
    margin_weight,
):
    fields, levels, row_count, col_count = state.shape
    slots = margin_row.shape[-1]
    ocean_comp = margin_row.shape[3] - 1
    part = slots // PARTS
    tiles = lax.axis_size("tile")
    comp = lax.axis_index("comp").astype(jnp.int32).reshape(1)
    counts = margin_count.reshape(3, ocean_comp + 1)
    scalar = pl.BlockSpec(memory_space=pltpu.SMEM)
    params = pltpu.CompilerParams(vmem_limit_bytes=VMEM_LIMIT)
    packet = jax.ShapeDtypeStruct((2 * PARTS, ocean_comp * part + LANES * HALO_ROWS // 8), jnp.float32)

    to_west, to_east = pl.pallas_call(
        functools.partial(edge_kernel, ocean_comp),
        in_specs=[scalar] + [pl.BlockSpec(memory_space=pl.ANY)] * 3,
        out_specs=[pl.BlockSpec(memory_space=pltpu.VMEM)] * 2,
        out_shape=[packet] * 2,
        scratch_shapes=[
            pltpu.VMEM(margin_row.shape, jnp.int32),
            pltpu.VMEM(margin_col.shape, jnp.int32),
            pltpu.VMEM((fields, 1, row_count, LANES), jnp.float32),
            pltpu.VMEM((fields, 1, row_count, LANES), jnp.float32),
            pltpu.VMEM((fields, levels, row_count, LANES), jnp.float32),
            pltpu.VMEM((fields, levels, row_count, LANES), jnp.float32),
            pltpu.SemaphoreType.DMA((6,)),
        ],
        compiler_params=pltpu.CompilerParams(vmem_limit_bytes=FIRST_VMEM_LIMIT),
        name="edge_gather",
    )(comp, margin_row, margin_col, state)
    forward = [(i, (i + 1) % tiles) for i in range(tiles)]
    backward = [(b, a) for a, b in forward]
    from_west = lax.ppermute(to_east, "tile", forward)
    from_east = lax.ppermute(to_west, "tile", backward)

    bundle = jax.ShapeDtypeStruct((3, 2 * PARTS, part), jnp.float32)
    centre = pl.pallas_call(
        functools.partial(centre_kernel, ocean_comp),
        grid=(1,),
        in_specs=[
            scalar,
            whole(margin_row),
            whole(margin_col),
            pl.BlockSpec((fields, 1, row_count, col_count), lambda i: (0, 0, 0, 0)),
        ],
        out_specs=whole(bundle),
        out_shape=bundle,
        compiler_params=params,
        name="centre_gather",
    )(comp, margin_row, margin_col, state)
    bundles = pl.pallas_call(
        functools.partial(pack_kernel, ocean_comp),
        grid=(1,),
        in_specs=[scalar, scalar, whole(bundle), whole(packet), whole(packet)],
        out_specs=[whole(bundle)] * ocean_comp,
        out_shape=[bundle] * ocean_comp,
        compiler_params=params,
        name="pack",
    )(comp, counts, centre, from_west, from_east)
    got = []
    for g in range(ocean_comp):
        swap = [(i, i ^ (g ^ ocean_comp)) for i in range(ocean_comp + 1)]
        got.append(lax.ppermute(bundles[g], "comp", swap))

    chunk = 32
    moved = pl.pallas_call(
        functools.partial(transport_kernel, ocean_comp * part),
        grid=(row_count // chunk,),
        in_specs=[
            pl.BlockSpec((fields, levels, chunk, col_count), lambda i: (0, 0, i, 0)),
            whole(courant),
            whole(mixing),
            whole(packet),
            whole(packet),
            pl.BlockSpec(memory_space=pl.ANY),
        ],
        out_specs=pl.BlockSpec((fields, levels, chunk, col_count), lambda i: (0, 0, i, 0)),
        out_shape=jax.ShapeDtypeStruct(state.shape, jnp.float32),
        scratch_shapes=[
            pltpu.VMEM((row_count, levels), jnp.float32),
            pltpu.VMEM((row_count, levels - 1), jnp.float32),
        ],
        compiler_params=params,
        name="transport",
    )(state, courant, mixing, from_west, from_east, bundles[0])

    surface_spec = pl.BlockSpec((fields, 1, row_count, col_count), lambda i: (0, 0, 0, 0))
    partner = jax.ShapeDtypeStruct((fields, row_count, col_count), jnp.float32)
    return pl.pallas_call(
        functools.partial(land_kernel, ocean_comp),
        grid=(1,),
        in_specs=[
            scalar,
            scalar,
            whole(margin_row),
            whole(margin_col),
            whole(margin_weight),
            whole(bundle),
            whole(bundle),
            whole(bundle),
            surface_spec,
            whole(exchange_coef),
            whole(sea_mask),
        ],
        out_specs=[surface_spec, whole(partner)],
        out_shape=[jax.ShapeDtypeStruct(state.shape, jnp.float32), partner],
        scratch_shapes=[
            pltpu.VMEM((2 * row_count, col_count), jnp.float32),
            pltpu.VMEM((row_count, 2 * LANES), jnp.float32),
            pltpu.VMEM((row_count, 2 * LANES), jnp.float32),
        ],
        input_output_aliases={8: 0},
        compiler_params=params,
        name="land",
    )(
        comp,
        counts,
        margin_row,
        margin_col,
        margin_weight,
        *got,
        moved,
        exchange_coef,
        sea_mask,
    )


def solution(mesh):
    in_specs = (
        P(None, None, "comp", "tile"),
        P(None, "comp"),
        P(None, "comp"),
        P("comp", "tile"),
        P("comp", "tile"),
        P("comp", "tile", None, None),
        P("comp", "tile", None, None, None),
        P("comp", "tile", None, None, None),
        P("comp", "tile", None, None, None),
    )
    out_specs = (P(None, None, "comp", "tile"), P(None, "comp", "tile"))
    return jax.shard_map(shards, mesh=mesh, in_specs=in_specs, out_specs=out_specs, check_vma=False)
```

```python
import functools
import jax
import jax.numpy as jnp
from jax import lax
from jax.experimental import pallas as pl
from jax.experimental.pallas import tpu as pltpu
from jax.sharding import PartitionSpec as P

SUBSTEPS = 2
LANES = 128
PARTS = 4
VMEM_LIMIT = 24 * 1024 * 1024
FIRST_VMEM_LIMIT = 60 * 1024 * 1024


def split_halves(values):
    high = values.astype(jnp.bfloat16)
    low = (values - high.astype(jnp.float32)).astype(jnp.bfloat16)
    return high, low


def one_hot(index_row, size):
    n = index_row.shape[1]
    inside = (index_row >= 0) & (index_row < size)
    number = jnp.where(inside, index_row, -1).astype(jnp.float32)
    number = jnp.broadcast_to(number, (16, n)).astype(jnp.bfloat16)
    blocks = []
    iota = lax.broadcasted_iota(jnp.int32, (16, n), 0).astype(jnp.float32)
    for block in range(size // 16):
        here = (iota + float(16 * block)).astype(jnp.bfloat16)
        blocks.append(jnp.where(number == here, jnp.bfloat16(1), jnp.bfloat16(0)))
    return jnp.concatenate(blocks, axis=0)


def one_hot_masks(index_row, size):
    n = index_row.shape[1]
    number = jnp.broadcast_to(index_row.astype(jnp.float32), (16, n)).astype(jnp.bfloat16)
    iota = lax.broadcasted_iota(jnp.int32, (16, n), 0).astype(jnp.float32)
    return [number == (iota + float(16 * block)).astype(jnp.bfloat16) for block in range(size // 16)]


def match_rows(total, rows):
    row_count = total.shape[0] // 2
    match = lax.broadcasted_iota(jnp.int32, (row_count, rows.shape[1]), 0) == rows
    first = jnp.sum(jnp.where(match, total[:row_count], 0.0), axis=0, keepdims=True)
    second = jnp.sum(jnp.where(match, total[row_count:], 0.0), axis=0, keepdims=True)
    return first, second


def wide_one_hot(columns, width):
    return jnp.concatenate(
        [one_hot(columns - start, min(256, width - start)) for start in range(0, width, 256)], axis=0
    )


def edge_kernel(
    ocean_comp,
    comp_ref,
    row_hbm,
    col_hbm,
    state_hbm,
    to_west,
    to_east,
    row_ref,
    col_ref,
    west_top,
    east_top,
    west_all,
    east_all,
    sems,
):
    ocean = comp_ref[0] == ocean_comp
    levels = west_all.shape[1]
    row_count = west_all.shape[2]
    part = row_ref.shape[-1] // PARTS
    cols = state_hbm.shape[3]
    near = slice(0, LANES)
    far = slice(cols - LANES, cols)
    copies = [
        pltpu.make_async_copy(source, target, sems.at[i])
        for i, (source, target) in enumerate(
            (
                (col_hbm, col_ref),
                (row_hbm, row_ref),
                (state_hbm.at[:, 0:1, :, near], west_top),
                (state_hbm.at[:, 0:1, :, far], east_top),
                (state_hbm.at[:, :, :, near], west_all),
                (state_hbm.at[:, :, :, far], east_all),
            )
        )
    ]
    for copy in copies:
        copy.start()
    sides = ((west_top, to_west, 0, 0), (east_top, to_east, 2, EAST_OFFSET))
    for copy in copies[:4]:
        copy.wait()

    def lists(pairs):
        for ref, out, o, offset in sides:
            high, low = split_halves(ref[:, 0].reshape(2 * row_count, LANES))
            surface = jnp.concatenate([high, low], axis=1)
            for slot, h in pairs:
                for q in range(PARTS):
                    span = slice(q * part, (q + 1) * part)
                    table = one_hot(col_ref[0, 0, o, h : h + 1, span] - offset, LANES)
                    total = jnp.dot(
                        surface,
                        jnp.concatenate([table, table], axis=0),
                        preferred_element_type=jnp.float32,
                    )
                    first, second = match_rows(total, row_ref[0, 0, o, h : h + 1, span])
                    out[q : q + 1, slot * part : (slot + 1) * part] = first
                    out[q + PARTS : q + PARTS + 1, slot * part : (slot + 1) * part] = second

    @pl.when(ocean)
    def _():
        lists([(j, j) for j in range(ocean_comp)])

    @pl.when(jnp.logical_not(ocean))
    def _():
        lists([(0, ocean_comp)])

    for copy in copies[4:]:
        copy.wait()
    lane = lax.broadcasted_iota(jnp.int32, (HALO_ROWS, LANES), 1)
    for ref, out, shift in ((west_all, to_west, 0), (east_all, to_east, 2)):
        tile = jnp.zeros((HALO_ROWS, LANES), jnp.float32)
        for group in range(row_count // HALO_ROWS):
            for k in range(2 * levels):
                at = 2 * k + group * HALO_LANES
                rows = ref[k // levels, k % levels, group * HALO_ROWS : (group + 1) * HALO_ROWS]
                tile = jnp.where(lane // 2 == at // 2, pltpu.roll(rows, (at + shift) % LANES, 1), tile)
        for block in range(HALO_ROWS // 8):
            start = ocean_comp * part + LANES * block
            out[:, start : start + LANES] = tile[8 * block : 8 * block + 8]


HALO_ROWS = 16
HALO_LANES = 32
EAST_OFFSET = 384


def centre_kernel(ocean_comp, comp_ref, row_ref, col_ref, state_ref, out):
    ocean = comp_ref[0] == ocean_comp
    row_count, col_count = state_ref.shape[2:]
    part = row_ref.shape[-1] // PARTS

    def lists(pairs):
        high, low = split_halves(state_ref[:, 0].reshape(2 * row_count, col_count))
        surface = jnp.concatenate([high, low], axis=0)
        for slot, h in pairs:
            for q in range(PARTS):
                span = slice(q * part, (q + 1) * part)
                table = wide_one_hot(col_ref[0, 0, 1, h : h + 1, span], col_count)
                total = jnp.dot(surface, table, preferred_element_type=jnp.float32)
                half = 2 * row_count
                first, second = match_rows(total[:half] + total[half:], row_ref[0, 0, 1, h : h + 1, span])
                out[slot, q : q + 1] = first
                out[slot, q + PARTS : q + PARTS + 1] = second

    @pl.when(ocean)
    def _():
        lists([(j, j) for j in range(ocean_comp)])

    @pl.when(jnp.logical_not(ocean))
    def _():
        lists([(0, ocean_comp)])


def pack_kernel(ocean_comp, comp_ref, count_ref, centre_ref, from_west, from_east, *outs):
    ocean = comp_ref[0] == ocean_comp
    part = centre_ref.shape[-1]

    def fill(slots):
        for slot, out in zip(slots, outs):
            span = slice(slot * part, (slot + 1) * part)
            out[0] = from_west[:, span]
            out[1] = centre_ref[slot]
            out[2] = from_east[:, span]

    @pl.when(ocean)
    def _():
        fill(range(ocean_comp))

    @pl.when(jnp.logical_not(ocean))
    def _():
        fill([0] * ocean_comp)


def transport_kernel(
    halo_start, state_ref, courant_ref, mixing_ref, west_ref, east_ref, unused_ref, out_ref, courant_by_row, mixing_by_row
):
    fields, levels, rows, cols = state_ref.shape
    step = pl.program_id(0)
    tiles = cols // LANES

    @pl.when(step == 0)
    def _():
        courant_by_row[...] = courant_ref[...].T
        mixing_by_row[...] = mixing_ref[...].T

    def spread(ref, level):
        here = pl.ds(pl.multiple_of(step * rows, 8), rows)
        return jnp.broadcast_to(ref[here, level : level + 1], (rows, LANES))[None]

    source = lax.broadcasted_iota(jnp.int32, (2 * LANES, 2 * LANES), 0) % LANES
    target = lax.broadcasted_iota(jnp.int32, (2 * LANES, 2 * LANES), 1)
    wanted = jnp.where(target < LANES, (target + LANES - 1) % LANES, (target + 1) % LANES)
    mover = jnp.where(source == wanted, 1.0, 0.0).astype(jnp.bfloat16)
    lane = lax.broadcasted_iota(jnp.int32, (levels, rows, LANES), 2)
    low_end = lane == 0
    high_end = lane == LANES - 1
    halo_lane = lax.broadcasted_iota(jnp.int32, (8, LANES), 1)

    speed = jnp.concatenate([spread(courant_by_row, level) for level in range(levels)], axis=0)
    half = 0.5 * speed
    square = half * speed
    middle, ahead, behind = 1.0 - 2.0 * square, square - half, square + half
    mix = jnp.concatenate([spread(mixing_by_row, level) for level in range(levels - 1)], axis=0)
    for f in range(fields):
        edges = []
        for level in range(levels):
            k = f * levels + level
            blocks = []
            for block in range(rows // 8):
                inner = 8 * block % HALO_ROWS // 8
                start = halo_start + inner * LANES
                group = step * (rows // HALO_ROWS) + 8 * block // HALO_ROWS
                at = 2 * k + group * HALO_LANES
                left = pltpu.roll(west_ref[:, start : start + LANES], (2 * LANES - 2 - at) % LANES, 1)
                right = pltpu.roll(east_ref[:, start : start + LANES], (LANES - at) % LANES, 1)
                blocks.append(jnp.where(halo_lane < LANES // 2, right, left))
            edges.append(jnp.concatenate(blocks, axis=0)[None])
        field = [state_ref[f, :, :, LANES * i : LANES * i + LANES] for i in range(tiles)]
        field.append(jnp.concatenate(edges, axis=0))
        for substep in range(SUBSTEPS):
            back, fore = [], []
            for tile in field:
                pair = jnp.concatenate(split_halves(tile.reshape(levels * rows, LANES)), axis=1)
                moved = jnp.dot(pair, mover, preferred_element_type=jnp.float32)
                back.append(moved[:, :LANES].reshape(tile.shape))
                fore.append(moved[:, LANES:].reshape(tile.shape))
            count = tiles if substep == SUBSTEPS - 1 else tiles + 1
            after = []
            for i in range(count):
                left = jnp.where(low_end, back[i - 1], back[i])
                right = jnp.where(high_end, fore[(i + 1) % (tiles + 1)], fore[i])
                q = field[i] * middle + right * ahead + left * behind
                flux = mix * (q[1:] - q[:-1])
                after.append(
                    jnp.concatenate([q[:1] + flux[:1], q[1:-1] + flux[1:] - flux[:-1], q[-1:] - flux[-1:]], axis=0)
                )
            field = after
        for i in range(tiles):
            out_ref[f, :, :, LANES * i : LANES * i + LANES] = field[i]


def land_kernel(
    ocean_comp,
    comp_ref,
    count_ref,
    row_ref,
    col_ref,
    weight_ref,
    got_0,
    got_1,
    got_2,
    field_hbm,
    coef_ref,
    mask_ref,
    state_hbm,
    partner_hbm,
    centre_ref,
    west_ref,
    east_ref,
    field_ref,
    state_out,
    partner_out,
    sems,
):
    fetch = pltpu.make_async_copy(field_hbm.at[:, 0:1], field_ref, sems.at[0])
    fetch.start()
    ocean = comp_ref[0] == ocean_comp
    row_count, col_count = coef_ref.shape
    part = row_ref.shape[-1] // PARTS
    slot_iota = lax.broadcasted_iota(jnp.int32, (1, part), 1)
    nt = (((1,), (1,)), ((), ()))

    def land(lists):
        for o, total_ref in ((1, centre_ref), (0, west_ref), (2, east_ref)):
            total = None
            for h, got in lists:
                count = count_ref[o, h]
                for q in range(PARTS):
                    span = slice(q * part, (q + 1) * part)
                    columns = col_ref[0, 0, o, h : h + 1, span]
                    rows = row_ref[0, 0, o, h : h + 1, span]
                    weights = weight_ref[0, 0, o, h : h + 1, span]
                    live = slot_iota + q * part < count
                    if o == 1:
                        table = wide_one_hot(columns, col_count)
                    else:
                        table = one_hot(columns - (EAST_OFFSET if o == 2 else 0), LANES)
                    masks = one_hot_masks(rows, row_count)
                    pieces = []
                    for f in range(2):
                        value = got[o, q + f * PARTS : q + f * PARTS + 1]
                        value = jnp.broadcast_to(jnp.where(live, weights * value, 0.0), (16, part))
                        pieces.append(split_halves(value))
                    left = jnp.concatenate(
                        [
                            jnp.where(mask, pieces[f][s], jnp.bfloat16(0))
                            for s in range(2)
                            for f in range(2)
                            for mask in masks
                        ],
                        axis=0,
                    )
                    product = lax.dot_general(left, table, nt, preferred_element_type=jnp.float32)
                    total = product if total is None else total + product
            size = total.shape[0] // 2
            total_ref[...] = total[:size] + total[size:]

    @pl.when(ocean)
    def _():
        land([(j, got) for j, got in enumerate((got_0, got_1, got_2))])

    @pl.when(jnp.logical_not(ocean))
    def _():
        comp = comp_ref[0]
        mine = jnp.where(comp == 0, got_0[...], jnp.where(comp == 1, got_1[...], got_2[...]))
        land([(ocean_comp, mine)])

    def far(f):
        centre = centre_ref[f * row_count : (f + 1) * row_count]
        sides = []
        for ref in (west_ref, east_ref):
            sides.append(ref[f * row_count : (f + 1) * row_count])
        return jnp.concatenate(
            [
                centre[:, :LANES] + sides[0],
                centre[:, LANES : col_count - LANES],
                centre[:, col_count - LANES :] + sides[1],
            ],
            axis=1,
        )

    first_far = far(0)
    second_far = far(1)
    partner_out[0] = first_far
    partner_out[1] = second_far
    send_partner = pltpu.make_async_copy(partner_out, partner_hbm, sems.at[1])
    send_partner.start()
    fetch.wait()
    rate = coef_ref[...] * mask_ref[...].astype(jnp.float32)
    first_own = field_ref[0, 0]
    second_own = field_ref[1, 0]
    state_out[0, 0] = first_own + rate * (first_far - first_own)
    air_second = second_own + rate * (1.2 * first_far - 0.3 * second_far - second_own)
    sea_second = second_own + rate * (1.2 * first_own - second_far)
    state_out[1, 0] = jnp.where(ocean, sea_second, air_second)
    send_state = pltpu.make_async_copy(state_out, state_hbm.at[:, 0:1], sems.at[2])
    send_state.start()
    send_partner.wait()
    send_state.wait()


def whole(array):
    return pl.BlockSpec(array.shape, functools.partial(lambda n, *i: (0,) * n, len(array.shape)))


def shards(
    state,
    courant,
    mixing,
    exchange_coef,
    sea_mask,
    margin_count,
    margin_row,
    margin_col,
    margin_weight,
):
    fields, levels, row_count, col_count = state.shape
    slots = margin_row.shape[-1]
    ocean_comp = margin_row.shape[3] - 1
    part = slots // PARTS
    tiles = lax.axis_size("tile")
    comp = lax.axis_index("comp").astype(jnp.int32).reshape(1)
    counts = margin_count.reshape(3, ocean_comp + 1)
    scalar = pl.BlockSpec(memory_space=pltpu.SMEM)
    params = pltpu.CompilerParams(vmem_limit_bytes=VMEM_LIMIT)
    packet = jax.ShapeDtypeStruct((2 * PARTS, ocean_comp * part + LANES * HALO_ROWS // 8), jnp.float32)

    to_west, to_east = pl.pallas_call(
        functools.partial(edge_kernel, ocean_comp),
        in_specs=[scalar] + [pl.BlockSpec(memory_space=pl.ANY)] * 3,
        out_specs=[pl.BlockSpec(memory_space=pltpu.VMEM)] * 2,
        out_shape=[packet] * 2,
        scratch_shapes=[
            pltpu.VMEM(margin_row.shape, jnp.int32),
            pltpu.VMEM(margin_col.shape, jnp.int32),
            pltpu.VMEM((fields, 1, row_count, LANES), jnp.float32),
            pltpu.VMEM((fields, 1, row_count, LANES), jnp.float32),
            pltpu.VMEM((fields, levels, row_count, LANES), jnp.float32),
            pltpu.VMEM((fields, levels, row_count, LANES), jnp.float32),
            pltpu.SemaphoreType.DMA((6,)),
        ],
        compiler_params=pltpu.CompilerParams(vmem_limit_bytes=FIRST_VMEM_LIMIT),
        name="edge_gather",
    )(comp, margin_row, margin_col, state)
    forward = [(i, (i + 1) % tiles) for i in range(tiles)]
    backward = [(b, a) for a, b in forward]
    from_west = lax.ppermute(to_east, "tile", forward)
    from_east = lax.ppermute(to_west, "tile", backward)

    bundle = jax.ShapeDtypeStruct((3, 2 * PARTS, part), jnp.float32)
    centre = pl.pallas_call(
        functools.partial(centre_kernel, ocean_comp),
        in_specs=[scalar] + [pl.BlockSpec(memory_space=pltpu.VMEM)] * 3,
        out_specs=pl.BlockSpec(memory_space=pltpu.VMEM),
        out_shape=bundle,
        compiler_params=params,
        name="centre_gather",
    )(comp, margin_row, margin_col, state)
    bundles = pl.pallas_call(
        functools.partial(pack_kernel, ocean_comp),
        in_specs=[scalar, scalar] + [pl.BlockSpec(memory_space=pltpu.VMEM)] * 3,
        out_specs=[pl.BlockSpec(memory_space=pltpu.VMEM)] * ocean_comp,
        out_shape=[bundle] * ocean_comp,
        compiler_params=params,
        name="pack",
    )(comp, counts, centre, from_west, from_east)
    got = []
    for g in range(ocean_comp):
        swap = [(i, i ^ (g ^ ocean_comp)) for i in range(ocean_comp + 1)]
        got.append(lax.ppermute(bundles[g], "comp", swap))

    chunk = 32
    moved = pl.pallas_call(
        functools.partial(transport_kernel, ocean_comp * part),
        grid=(row_count // chunk,),
        in_specs=[
            pl.BlockSpec((fields, levels, chunk, col_count), lambda i: (0, 0, i, 0)),
            whole(courant),
            whole(mixing),
            whole(packet),
            whole(packet),
            pl.BlockSpec(memory_space=pl.ANY),
        ],
        out_specs=pl.BlockSpec((fields, levels, chunk, col_count), lambda i: (0, 0, i, 0)),
        out_shape=jax.ShapeDtypeStruct(state.shape, jnp.float32),
        scratch_shapes=[
            pltpu.VMEM((row_count, levels), jnp.float32),
            pltpu.VMEM((row_count, levels - 1), jnp.float32),
        ],
        compiler_params=params,
        name="transport",
    )(state, courant, mixing, from_west, from_east, bundles[0])

    level = (fields, 1, row_count, col_count)
    partner = jax.ShapeDtypeStruct((fields, row_count, col_count), jnp.float32)
    local = pl.BlockSpec(memory_space=pltpu.VMEM)
    anywhere = pl.BlockSpec(memory_space=pl.ANY)
    return pl.pallas_call(
        functools.partial(land_kernel, ocean_comp),
        in_specs=[scalar, scalar] + [local] * 6 + [anywhere, local, local],
        out_specs=[anywhere, anywhere],
        out_shape=[jax.ShapeDtypeStruct(state.shape, jnp.float32), partner],
        scratch_shapes=[
            pltpu.VMEM((2 * row_count, col_count), jnp.float32),
            pltpu.VMEM((2 * row_count, LANES), jnp.float32),
            pltpu.VMEM((2 * row_count, LANES), jnp.float32),
            pltpu.VMEM(level, jnp.float32),
            pltpu.VMEM(level, jnp.float32),
            pltpu.VMEM(partner.shape, jnp.float32),
            pltpu.SemaphoreType.DMA((3,)),
        ],
        input_output_aliases={8: 0},
        compiler_params=params,
        name="land",
    )(
        comp,
        counts,
        margin_row,
        margin_col,
        margin_weight,
        *got,
        moved,
        exchange_coef,
        sea_mask,
    )


def solution(mesh):
    in_specs = (
        P(None, None, "comp", "tile"),
        P(None, "comp"),
        P(None, "comp"),
        P("comp", "tile"),
        P("comp", "tile"),
        P("comp", "tile", None, None),
        P("comp", "tile", None, None, None),
        P("comp", "tile", None, None, None),
        P("comp", "tile", None, None, None),
    )
    out_specs = (P(None, None, "comp", "tile"), P(None, "comp", "tile"))
    return jax.shard_map(shards, mesh=mesh, in_specs=in_specs, out_specs=out_specs, check_vma=False)
```

```python
import functools
import jax
import jax.numpy as jnp
from jax import lax
from jax.experimental import pallas as pl
from jax.experimental.pallas import tpu as pltpu
from jax.sharding import PartitionSpec as P

SUBSTEPS = 2
LANES = 128
PARTS = 4
VMEM_LIMIT = 24 * 1024 * 1024
FIRST_VMEM_LIMIT = 60 * 1024 * 1024


def split_halves(values):
    high = values.astype(jnp.bfloat16)
    low = (values - high.astype(jnp.float32)).astype(jnp.bfloat16)
    return high, low


def one_hot(index_row, size):
    n = index_row.shape[1]
    inside = (index_row >= 0) & (index_row < size)
    number = jnp.where(inside, index_row, -1).astype(jnp.float32)
    number = jnp.broadcast_to(number, (16, n)).astype(jnp.bfloat16)
    blocks = []
    iota = lax.broadcasted_iota(jnp.int32, (16, n), 0).astype(jnp.float32)
    for block in range(size // 16):
        here = (iota + float(16 * block)).astype(jnp.bfloat16)
        blocks.append(jnp.where(number == here, jnp.bfloat16(1), jnp.bfloat16(0)))
    return jnp.concatenate(blocks, axis=0)


def one_hot_masks(index_row, size):
    n = index_row.shape[1]
    number = jnp.broadcast_to(index_row.astype(jnp.float32), (16, n)).astype(jnp.bfloat16)
    iota = lax.broadcasted_iota(jnp.int32, (16, n), 0).astype(jnp.float32)
    return [number == (iota + float(16 * block)).astype(jnp.bfloat16) for block in range(size // 16)]


def match_rows(total, rows):
    row_count = total.shape[0] // 2
    match = lax.broadcasted_iota(jnp.int32, (row_count, rows.shape[1]), 0) == rows
    first = jnp.sum(jnp.where(match, total[:row_count], 0.0), axis=0, keepdims=True)
    second = jnp.sum(jnp.where(match, total[row_count:], 0.0), axis=0, keepdims=True)
    return first, second


def wide_one_hot(columns, width):
    return jnp.concatenate(
        [one_hot(columns - start, min(256, width - start)) for start in range(0, width, 256)], axis=0
    )


def edge_kernel(
    ocean_comp,
    comp_ref,
    row_hbm,
    col_hbm,
    state_hbm,
    to_west,
    to_east,
    row_ref,
    col_ref,
    west_top,
    east_top,
    west_all,
    east_all,
    sems,
):
    ocean = comp_ref[0] == ocean_comp
    levels = west_all.shape[1]
    row_count = west_all.shape[2]
    part = row_ref.shape[-1] // PARTS
    cols = state_hbm.shape[3]
    near = slice(0, LANES)
    far = slice(cols - LANES, cols)
    copies = [
        pltpu.make_async_copy(source, target, sems.at[i])
        for i, (source, target) in enumerate(
            (
                (col_hbm, col_ref),
                (row_hbm, row_ref),
                (state_hbm.at[:, 0:1, :, near], west_top),
                (state_hbm.at[:, 0:1, :, far], east_top),
                (state_hbm.at[:, :, :, near], west_all),
                (state_hbm.at[:, :, :, far], east_all),
            )
        )
    ]
    for copy in copies:
        copy.start()
    sides = ((west_top, to_west, 0, 0), (east_top, to_east, 2, EAST_OFFSET))
    for copy in copies[:4]:
        copy.wait()

    def lists(pairs):
        for ref, out, o, offset in sides:
            high, low = split_halves(ref[:, 0].reshape(2 * row_count, LANES))
            surface = jnp.concatenate([high, low], axis=1)
            for slot, h in pairs:
                for q in range(PARTS):
                    span = slice(q * part, (q + 1) * part)
                    table = one_hot(col_ref[0, 0, o, h : h + 1, span] - offset, LANES)
                    total = jnp.dot(
                        surface,
                        jnp.concatenate([table, table], axis=0),
                        preferred_element_type=jnp.float32,
                    )
                    first, second = match_rows(total, row_ref[0, 0, o, h : h + 1, span])
                    out[q : q + 1, slot * part : (slot + 1) * part] = first
                    out[q + PARTS : q + PARTS + 1, slot * part : (slot + 1) * part] = second

    @pl.when(ocean)
    def _():
        lists([(j, j) for j in range(ocean_comp)])

    @pl.when(jnp.logical_not(ocean))
    def _():
        lists([(0, ocean_comp)])

    for copy in copies[4:]:
        copy.wait()
    lane = lax.broadcasted_iota(jnp.int32, (HALO_ROWS, LANES), 1)
    for ref, out, shift in ((west_all, to_west, 0), (east_all, to_east, 2)):
        tile = jnp.zeros((HALO_ROWS, LANES), jnp.float32)
        for group in range(row_count // HALO_ROWS):
            for k in range(2 * levels):
                at = 2 * k + group * HALO_LANES
                rows = ref[k // levels, k % levels, group * HALO_ROWS : (group + 1) * HALO_ROWS]
                tile = jnp.where(lane // 2 == at // 2, pltpu.roll(rows, (at + shift) % LANES, 1), tile)
        for block in range(HALO_ROWS // 8):
            start = ocean_comp * part + LANES * block
            out[:, start : start + LANES] = tile[8 * block : 8 * block + 8]


HALO_ROWS = 16
HALO_LANES = 32
EAST_OFFSET = 384


def centre_kernel(ocean_comp, comp_ref, row_ref, col_ref, state_ref, out):
    ocean = comp_ref[0] == ocean_comp
    row_count, col_count = state_ref.shape[2:]
    part = row_ref.shape[-1] // PARTS

    def lists(pairs):
        high, low = split_halves(state_ref[:, 0].reshape(2 * row_count, col_count))
        surface = jnp.concatenate([high, low], axis=0)
        for slot, h in pairs:
            for q in range(PARTS):
                span = slice(q * part, (q + 1) * part)
                table = wide_one_hot(col_ref[0, 0, 1, h : h + 1, span], col_count)
                total = jnp.dot(surface, table, preferred_element_type=jnp.float32)
                half = 2 * row_count
                first, second = match_rows(total[:half] + total[half:], row_ref[0, 0, 1, h : h + 1, span])
                out[slot, q : q + 1] = first
                out[slot, q + PARTS : q + PARTS + 1] = second

    @pl.when(ocean)
    def _():
        lists([(j, j) for j in range(ocean_comp)])

    @pl.when(jnp.logical_not(ocean))
    def _():
        lists([(0, ocean_comp)])


def pack_kernel(ocean_comp, comp_ref, count_ref, centre_ref, from_west, from_east, *outs):
    ocean = comp_ref[0] == ocean_comp
    part = centre_ref.shape[-1]

    def fill(slots):
        for slot, out in zip(slots, outs):
            span = slice(slot * part, (slot + 1) * part)
            out[0] = from_west[:, span]
            out[1] = centre_ref[slot]
            out[2] = from_east[:, span]

    @pl.when(ocean)
    def _():
        fill(range(ocean_comp))

    @pl.when(jnp.logical_not(ocean))
    def _():
        fill([0] * ocean_comp)


def transport_kernel(
    halo_start, state_ref, courant_ref, mixing_ref, west_ref, east_ref, unused_ref, out_hbm, out_ref, sems
):
    fields, levels, rows, cols = state_ref.shape
    tiles = cols // LANES
    courant_by_row = courant_ref[...].T
    mixing_by_row = mixing_ref[...].T

    def spread(table, level):
        return jnp.broadcast_to(table[:, level : level + 1], (rows, LANES))[None]

    source = lax.broadcasted_iota(jnp.int32, (2 * LANES, 2 * LANES), 0) % LANES
    target = lax.broadcasted_iota(jnp.int32, (2 * LANES, 2 * LANES), 1)
    wanted = jnp.where(target < LANES, (target + LANES - 1) % LANES, (target + 1) % LANES)
    mover = jnp.where(source == wanted, 1.0, 0.0).astype(jnp.bfloat16)
    lane = lax.broadcasted_iota(jnp.int32, (levels, rows, LANES), 2)
    low_end = lane == 0
    high_end = lane == LANES - 1
    halo_lane = lax.broadcasted_iota(jnp.int32, (8, LANES), 1)

    speed = jnp.concatenate([spread(courant_by_row, level) for level in range(levels)], axis=0)
    half = 0.5 * speed
    square = half * speed
    middle, ahead, behind = 1.0 - 2.0 * square, square - half, square + half
    mix = jnp.concatenate([spread(mixing_by_row, level) for level in range(levels - 1)], axis=0)
    copies = []
    for f in range(fields):
        edges = []
        for level in range(levels):
            k = f * levels + level
            blocks = []
            for block in range(rows // 8):
                inner = 8 * block % HALO_ROWS // 8
                start = halo_start + inner * LANES
                group = 8 * block // HALO_ROWS
                at = 2 * k + group * HALO_LANES
                left = pltpu.roll(west_ref[:, start : start + LANES], (2 * LANES - 2 - at) % LANES, 1)
                right = pltpu.roll(east_ref[:, start : start + LANES], (LANES - at) % LANES, 1)
                blocks.append(jnp.where(halo_lane < LANES // 2, right, left))
            edges.append(jnp.concatenate(blocks, axis=0)[None])
        field = [state_ref[f, :, :, LANES * i : LANES * i + LANES] for i in range(tiles)]
        field.append(jnp.concatenate(edges, axis=0))
        for substep in range(SUBSTEPS):
            back, fore = [], []
            for tile in field:
                pair = jnp.concatenate(split_halves(tile.reshape(levels * rows, LANES)), axis=1)
                moved = jnp.dot(pair, mover, preferred_element_type=jnp.float32)
                back.append(moved[:, :LANES].reshape(tile.shape))
                fore.append(moved[:, LANES:].reshape(tile.shape))
            count = tiles if substep == SUBSTEPS - 1 else tiles + 1
            after = []
            for i in range(count):
                left = jnp.where(low_end, back[i - 1], back[i])
                right = jnp.where(high_end, fore[(i + 1) % (tiles + 1)], fore[i])
                q = field[i] * middle + right * ahead + left * behind
                flux = mix * (q[1:] - q[:-1])
                after.append(
                    jnp.concatenate([q[:1] + flux[:1], q[1:-1] + flux[1:] - flux[:-1], q[-1:] - flux[-1:]], axis=0)
                )
            field = after
        for i in range(tiles):
            out_ref[f, :, :, LANES * i : LANES * i + LANES] = field[i]
        copies.append(pltpu.make_async_copy(out_ref.at[f : f + 1], out_hbm.at[f : f + 1], sems.at[f]))
        copies[f].start()
    for copy in copies:
        copy.wait()


def land_kernel(
    ocean_comp,
    comp_ref,
    count_ref,
    row_ref,
    col_ref,
    weight_ref,
    got_0,
    got_1,
    got_2,
    field_hbm,
    coef_ref,
    mask_ref,
    state_hbm,
    partner_hbm,
    centre_ref,
    west_ref,
    east_ref,
    field_ref,
    state_out,
    partner_out,
    sems,
):
    fetch = pltpu.make_async_copy(field_hbm.at[:, 0:1], field_ref, sems.at[0])
    fetch.start()
    ocean = comp_ref[0] == ocean_comp
    row_count, col_count = coef_ref.shape
    part = row_ref.shape[-1] // PARTS
    slot_iota = lax.broadcasted_iota(jnp.int32, (1, part), 1)
    nt = (((1,), (1,)), ((), ()))

    def land(lists):
        for o, total_ref in ((1, centre_ref), (0, west_ref), (2, east_ref)):
            total = None
            for h, got in lists:
                count = count_ref[o, h]
                for q in range(PARTS):
                    span = slice(q * part, (q + 1) * part)
                    columns = col_ref[0, 0, o, h : h + 1, span]
                    rows = row_ref[0, 0, o, h : h + 1, span]
                    weights = weight_ref[0, 0, o, h : h + 1, span]
                    live = slot_iota + q * part < count
                    if o == 1:
                        table = wide_one_hot(columns, col_count)
                    else:
                        table = one_hot(columns - (EAST_OFFSET if o == 2 else 0), LANES)
                    masks = one_hot_masks(rows, row_count)
                    pieces = []
                    for f in range(2):
                        value = got[o, q + f * PARTS : q + f * PARTS + 1]
                        value = jnp.broadcast_to(jnp.where(live, weights * value, 0.0), (16, part))
                        pieces.append(split_halves(value))
                    left = jnp.concatenate(
                        [
                            jnp.where(mask, pieces[f][s], jnp.bfloat16(0))
                            for s in range(2)
                            for f in range(2)
                            for mask in masks
                        ],
                        axis=0,
                    )
                    product = lax.dot_general(left, table, nt, preferred_element_type=jnp.float32)
                    total = product if total is None else total + product
            size = total.shape[0] // 2
            total_ref[...] = total[:size] + total[size:]

    @pl.when(ocean)
    def _():
        land([(j, got) for j, got in enumerate((got_0, got_1, got_2))])

    @pl.when(jnp.logical_not(ocean))
    def _():
        comp = comp_ref[0]
        mine = jnp.where(comp == 0, got_0[...], jnp.where(comp == 1, got_1[...], got_2[...]))
        land([(ocean_comp, mine)])

    def far(f):
        centre = centre_ref[f * row_count : (f + 1) * row_count]
        sides = []
        for ref in (west_ref, east_ref):
            sides.append(ref[f * row_count : (f + 1) * row_count])
        return jnp.concatenate(
            [
                centre[:, :LANES] + sides[0],
                centre[:, LANES : col_count - LANES],
                centre[:, col_count - LANES :] + sides[1],
            ],
            axis=1,
        )

    first_far = far(0)
    second_far = far(1)
    partner_out[0] = first_far
    partner_out[1] = second_far
    send_partner = pltpu.make_async_copy(partner_out, partner_hbm, sems.at[1])
    send_partner.start()
    fetch.wait()
    rate = coef_ref[...] * mask_ref[...].astype(jnp.float32)
    first_own = field_ref[0, 0]
    second_own = field_ref[1, 0]
    state_out[0, 0] = first_own + rate * (first_far - first_own)
    air_second = second_own + rate * (1.2 * first_far - 0.3 * second_far - second_own)
    sea_second = second_own + rate * (1.2 * first_own - second_far)
    state_out[1, 0] = jnp.where(ocean, sea_second, air_second)
    send_state = pltpu.make_async_copy(state_out, state_hbm.at[:, 0:1], sems.at[2])
    send_state.start()
    send_partner.wait()
    send_state.wait()


def whole(array):
    return pl.BlockSpec(array.shape, functools.partial(lambda n, *i: (0,) * n, len(array.shape)))


def shards(
    state,
    courant,
    mixing,
    exchange_coef,
    sea_mask,
    margin_count,
    margin_row,
    margin_col,
    margin_weight,
):
    fields, levels, row_count, col_count = state.shape
    slots = margin_row.shape[-1]
    ocean_comp = margin_row.shape[3] - 1
    part = slots // PARTS
    tiles = lax.axis_size("tile")
    comp = lax.axis_index("comp").astype(jnp.int32).reshape(1)
    counts = margin_count.reshape(3, ocean_comp + 1)
    scalar = pl.BlockSpec(memory_space=pltpu.SMEM)
    params = pltpu.CompilerParams(vmem_limit_bytes=VMEM_LIMIT)
    packet = jax.ShapeDtypeStruct((2 * PARTS, ocean_comp * part + LANES * HALO_ROWS // 8), jnp.float32)

    to_west, to_east = pl.pallas_call(
        functools.partial(edge_kernel, ocean_comp),
        in_specs=[scalar] + [pl.BlockSpec(memory_space=pl.ANY)] * 3,
        out_specs=[pl.BlockSpec(memory_space=pltpu.VMEM)] * 2,
        out_shape=[packet] * 2,
        scratch_shapes=[
            pltpu.VMEM(margin_row.shape, jnp.int32),
            pltpu.VMEM(margin_col.shape, jnp.int32),
            pltpu.VMEM((fields, 1, row_count, LANES), jnp.float32),
            pltpu.VMEM((fields, 1, row_count, LANES), jnp.float32),
            pltpu.VMEM((fields, levels, row_count, LANES), jnp.float32),
            pltpu.VMEM((fields, levels, row_count, LANES), jnp.float32),
            pltpu.SemaphoreType.DMA((6,)),
        ],
        compiler_params=pltpu.CompilerParams(vmem_limit_bytes=FIRST_VMEM_LIMIT),
        name="edge_gather",
    )(comp, margin_row, margin_col, state)
    forward = [(i, (i + 1) % tiles) for i in range(tiles)]
    backward = [(b, a) for a, b in forward]
    from_west = lax.ppermute(to_east, "tile", forward)
    from_east = lax.ppermute(to_west, "tile", backward)

    bundle = jax.ShapeDtypeStruct((3, 2 * PARTS, part), jnp.float32)
    centre = pl.pallas_call(
        functools.partial(centre_kernel, ocean_comp),
        in_specs=[scalar] + [pl.BlockSpec(memory_space=pltpu.VMEM)] * 3,
        out_specs=pl.BlockSpec(memory_space=pltpu.VMEM),
        out_shape=bundle,
        compiler_params=params,
        name="centre_gather",
    )(comp, margin_row, margin_col, state)
    bundles = pl.pallas_call(
        functools.partial(pack_kernel, ocean_comp),
        in_specs=[scalar, scalar] + [pl.BlockSpec(memory_space=pltpu.VMEM)] * 3,
        out_specs=[pl.BlockSpec(memory_space=pltpu.VMEM)] * ocean_comp,
        out_shape=[bundle] * ocean_comp,
        compiler_params=params,
        name="pack",
    )(comp, counts, centre, from_west, from_east)
    got = []
    for g in range(ocean_comp):
        swap = [(i, i ^ (g ^ ocean_comp)) for i in range(ocean_comp + 1)]
        got.append(lax.ppermute(bundles[g], "comp", swap))

    moved = pl.pallas_call(
        functools.partial(transport_kernel, ocean_comp * part),
        in_specs=[pl.BlockSpec(memory_space=pltpu.VMEM)] * 5 + [pl.BlockSpec(memory_space=pl.ANY)],
        out_specs=pl.BlockSpec(memory_space=pl.ANY),
        out_shape=jax.ShapeDtypeStruct(state.shape, jnp.float32),
        scratch_shapes=[pltpu.VMEM(state.shape, jnp.float32), pltpu.SemaphoreType.DMA((fields,))],
        compiler_params=params,
        name="transport",
    )(state, courant, mixing, from_west, from_east, bundles[0])

    level = (fields, 1, row_count, col_count)
    partner = jax.ShapeDtypeStruct((fields, row_count, col_count), jnp.float32)
    local = pl.BlockSpec(memory_space=pltpu.VMEM)
    anywhere = pl.BlockSpec(memory_space=pl.ANY)
    return pl.pallas_call(
        functools.partial(land_kernel, ocean_comp),
        in_specs=[scalar, scalar] + [local] * 6 + [anywhere, local, local],
        out_specs=[anywhere, anywhere],
        out_shape=[jax.ShapeDtypeStruct(state.shape, jnp.float32), partner],
        scratch_shapes=[
            pltpu.VMEM((2 * row_count, col_count), jnp.float32),
            pltpu.VMEM((2 * row_count, LANES), jnp.float32),
            pltpu.VMEM((2 * row_count, LANES), jnp.float32),
            pltpu.VMEM(level, jnp.float32),
            pltpu.VMEM(level, jnp.float32),
            pltpu.VMEM(partner.shape, jnp.float32),
            pltpu.SemaphoreType.DMA((3,)),
        ],
        input_output_aliases={8: 0},
        compiler_params=params,
        name="land",
    )(
        comp,
        counts,
        margin_row,
        margin_col,
        margin_weight,
        *got,
        moved,
        exchange_coef,
        sea_mask,
    )


def solution(mesh):
    in_specs = (
        P(None, None, "comp", "tile"),
        P(None, "comp"),
        P(None, "comp"),
        P("comp", "tile"),
        P("comp", "tile"),
        P("comp", "tile", None, None),
        P("comp", "tile", None, None, None),
        P("comp", "tile", None, None, None),
        P("comp", "tile", None, None, None),
    )
    out_specs = (P(None, None, "comp", "tile"), P(None, "comp", "tile"))
    return jax.shard_map(shards, mesh=mesh, in_specs=in_specs, out_specs=out_specs, check_vma=False)
```

```python
import functools
import jax
import jax.numpy as jnp
from jax import lax
from jax.experimental import pallas as pl
from jax.experimental.pallas import tpu as pltpu
from jax.sharding import PartitionSpec as P

SUBSTEPS = 2
LANES = 128
PARTS = 4
VMEM_LIMIT = 24 * 1024 * 1024
FIRST_VMEM_LIMIT = 60 * 1024 * 1024


def split_halves(values):
    high = values.astype(jnp.bfloat16)
    low = (values - high.astype(jnp.float32)).astype(jnp.bfloat16)
    return high, low


def one_hot(index_row, size):
    n = index_row.shape[1]
    inside = (index_row >= 0) & (index_row < size)
    number = jnp.where(inside, index_row, -1).astype(jnp.float32)
    number = jnp.broadcast_to(number, (16, n)).astype(jnp.bfloat16)
    blocks = []
    iota = lax.broadcasted_iota(jnp.int32, (16, n), 0).astype(jnp.float32)
    for block in range(size // 16):
        here = (iota + float(16 * block)).astype(jnp.bfloat16)
        blocks.append(jnp.where(number == here, jnp.bfloat16(1), jnp.bfloat16(0)))
    return jnp.concatenate(blocks, axis=0)


def one_hot_masks(index_row, size):
    n = index_row.shape[1]
    number = jnp.broadcast_to(index_row.astype(jnp.float32), (16, n)).astype(jnp.bfloat16)
    iota = lax.broadcasted_iota(jnp.int32, (16, n), 0).astype(jnp.float32)
    return [number == (iota + float(16 * block)).astype(jnp.bfloat16) for block in range(size // 16)]


def match_rows(total, rows):
    row_count = total.shape[0] // 2
    match = lax.broadcasted_iota(jnp.int32, (row_count, rows.shape[1]), 0) == rows
    first = jnp.sum(jnp.where(match, total[:row_count], 0.0), axis=0, keepdims=True)
    second = jnp.sum(jnp.where(match, total[row_count:], 0.0), axis=0, keepdims=True)
    return first, second


def wide_one_hot(columns, width):
    return jnp.concatenate(
        [one_hot(columns - start, min(256, width - start)) for start in range(0, width, 256)], axis=0
    )


def edge_kernel(
    ocean_comp,
    comp_ref,
    row_hbm,
    col_hbm,
    state_hbm,
    to_west,
    to_east,
    row_ref,
    col_ref,
    west_top,
    east_top,
    west_all,
    east_all,
    sems,
):
    ocean = comp_ref[0] == ocean_comp
    levels = west_all.shape[1]
    row_count = west_all.shape[2]
    part = row_ref.shape[-1] // PARTS
    cols = state_hbm.shape[3]
    near = slice(0, LANES)
    far = slice(cols - LANES, cols)
    copies = [
        pltpu.make_async_copy(source, target, sems.at[i])
        for i, (source, target) in enumerate(
            (
                (col_hbm.at[:, :, 0:1], col_ref.at[:, :, 0:1]),
                (row_hbm.at[:, :, 0:1], row_ref.at[:, :, 0:1]),
                (state_hbm.at[:, 0:1, :, near], west_top),
                (col_hbm.at[:, :, 2:3], col_ref.at[:, :, 2:3]),
                (row_hbm.at[:, :, 2:3], row_ref.at[:, :, 2:3]),
                (state_hbm.at[:, 0:1, :, far], east_top),
                (state_hbm.at[:, :, :, near], west_all),
                (state_hbm.at[:, :, :, far], east_all),
            )
        )
    ]
    for copy in copies:
        copy.start()
    sides = ((west_top, to_west, 0, 0), (east_top, to_east, 2, EAST_OFFSET))
    for copy in copies[:3]:
        copy.wait()

    def lists(pairs):
        for ref, out, o, offset in sides:
            if o == 2:
                for copy in copies[3:6]:
                    copy.wait()
            high, low = split_halves(ref[:, 0].reshape(2 * row_count, LANES))
            surface = jnp.concatenate([high, low], axis=1)
            for slot, h in pairs:
                for q in range(PARTS):
                    span = slice(q * part, (q + 1) * part)
                    table = one_hot(col_ref[0, 0, o, h : h + 1, span] - offset, LANES)
                    total = jnp.dot(
                        surface,
                        jnp.concatenate([table, table], axis=0),
                        preferred_element_type=jnp.float32,
                    )
                    first, second = match_rows(total, row_ref[0, 0, o, h : h + 1, span])
                    out[q : q + 1, slot * part : (slot + 1) * part] = first
                    out[q + PARTS : q + PARTS + 1, slot * part : (slot + 1) * part] = second

    @pl.when(ocean)
    def _():
        lists([(j, j) for j in range(ocean_comp)])

    @pl.when(jnp.logical_not(ocean))
    def _():
        lists([(0, ocean_comp)])

    for copy in copies[6:]:
        copy.wait()
    lane = lax.broadcasted_iota(jnp.int32, (HALO_ROWS, LANES), 1)
    for ref, out, shift in ((west_all, to_west, 0), (east_all, to_east, 2)):
        tile = jnp.zeros((HALO_ROWS, LANES), jnp.float32)
        for group in range(row_count // HALO_ROWS):
            for k in range(2 * levels):
                at = 2 * k + group * HALO_LANES
                rows = ref[k // levels, k % levels, group * HALO_ROWS : (group + 1) * HALO_ROWS]
                tile = jnp.where(lane // 2 == at // 2, pltpu.roll(rows, (at + shift) % LANES, 1), tile)
        for block in range(HALO_ROWS // 8):
            start = ocean_comp * part + LANES * block
            out[:, start : start + LANES] = tile[8 * block : 8 * block + 8]


HALO_ROWS = 16
HALO_LANES = 32
EAST_OFFSET = 384


def centre_kernel(ocean_comp, comp_ref, row_ref, col_ref, state_ref, out):
    ocean = comp_ref[0] == ocean_comp
    row_count, col_count = state_ref.shape[2:]
    part = row_ref.shape[-1] // PARTS

    def lists(pairs):
        high, low = split_halves(state_ref[:, 0].reshape(2 * row_count, col_count))
        surface = jnp.concatenate([high, low], axis=0)
        for slot, h in pairs:
            for q in range(PARTS):
                span = slice(q * part, (q + 1) * part)
                table = wide_one_hot(col_ref[0, 0, 1, h : h + 1, span], col_count)
                total = jnp.dot(surface, table, preferred_element_type=jnp.float32)
                half = 2 * row_count
                first, second = match_rows(total[:half] + total[half:], row_ref[0, 0, 1, h : h + 1, span])
                out[slot, q : q + 1] = first
                out[slot, q + PARTS : q + PARTS + 1] = second

    @pl.when(ocean)
    def _():
        lists([(j, j) for j in range(ocean_comp)])

    @pl.when(jnp.logical_not(ocean))
    def _():
        lists([(0, ocean_comp)])


def pack_kernel(ocean_comp, comp_ref, count_ref, centre_ref, from_west, from_east, *outs):
    ocean = comp_ref[0] == ocean_comp
    part = centre_ref.shape[-1]

    def fill(slots):
        for slot, out in zip(slots, outs):
            span = slice(slot * part, (slot + 1) * part)
            out[0] = from_west[:, span]
            out[1] = centre_ref[slot]
            out[2] = from_east[:, span]

    @pl.when(ocean)
    def _():
        fill(range(ocean_comp))

    @pl.when(jnp.logical_not(ocean))
    def _():
        fill([0] * ocean_comp)


def transport_kernel(
    halo_start, state_ref, courant_ref, mixing_ref, west_ref, east_ref, unused_ref, out_hbm, out_ref, sems
):
    fields, levels, rows, cols = state_ref.shape
    tiles = cols // LANES
    courant_by_row = courant_ref[...].T
    mixing_by_row = mixing_ref[...].T

    def spread(table, level):
        return jnp.broadcast_to(table[:, level : level + 1], (rows, LANES))[None]

    source = lax.broadcasted_iota(jnp.int32, (2 * LANES, 2 * LANES), 0) % LANES
    target = lax.broadcasted_iota(jnp.int32, (2 * LANES, 2 * LANES), 1)
    wanted = jnp.where(target < LANES, (target + LANES - 1) % LANES, (target + 1) % LANES)
    mover = jnp.where(source == wanted, 1.0, 0.0).astype(jnp.bfloat16)
    lane = lax.broadcasted_iota(jnp.int32, (levels, rows, LANES), 2)
    low_end = lane == 0
    high_end = lane == LANES - 1
    halo_lane = lax.broadcasted_iota(jnp.int32, (8, LANES), 1)

    speed = jnp.concatenate([spread(courant_by_row, level) for level in range(levels)], axis=0)
    half = 0.5 * speed
    square = half * speed
    middle, ahead, behind = 1.0 - 2.0 * square, square - half, square + half
    mix = jnp.concatenate([spread(mixing_by_row, level) for level in range(levels - 1)], axis=0)
    copies = []
    for f in range(fields):
        edges = []
        for level in range(levels):
            k = f * levels + level
            blocks = []
            for block in range(rows // 8):
                inner = 8 * block % HALO_ROWS // 8
                start = halo_start + inner * LANES
                group = 8 * block // HALO_ROWS
                at = 2 * k + group * HALO_LANES
                left = pltpu.roll(west_ref[:, start : start + LANES], (2 * LANES - 2 - at) % LANES, 1)
                right = pltpu.roll(east_ref[:, start : start + LANES], (LANES - at) % LANES, 1)
                blocks.append(jnp.where(halo_lane < LANES // 2, right, left))
            edges.append(jnp.concatenate(blocks, axis=0)[None])
        field = [state_ref[f, :, :, LANES * i : LANES * i + LANES] for i in range(tiles)]
        field.append(jnp.concatenate(edges, axis=0))
        for substep in range(SUBSTEPS):
            back, fore = [], []
            for tile in field:
                pair = jnp.concatenate(split_halves(tile.reshape(levels * rows, LANES)), axis=1)
                moved = jnp.dot(pair, mover, preferred_element_type=jnp.float32)
                back.append(moved[:, :LANES].reshape(tile.shape))
                fore.append(moved[:, LANES:].reshape(tile.shape))
            count = tiles if substep == SUBSTEPS - 1 else tiles + 1
            after = []
            for i in range(count):
                left = jnp.where(low_end, back[i - 1], back[i])
                right = jnp.where(high_end, fore[(i + 1) % (tiles + 1)], fore[i])
                q = field[i] * middle + right * ahead + left * behind
                flux = mix * (q[1:] - q[:-1])
                after.append(
                    jnp.concatenate([q[:1] + flux[:1], q[1:-1] + flux[1:] - flux[:-1], q[-1:] - flux[-1:]], axis=0)
                )
            field = after
        for i in range(tiles):
            out_ref[f, :, :, LANES * i : LANES * i + LANES] = field[i]
        copies.append(pltpu.make_async_copy(out_ref.at[f : f + 1], out_hbm.at[f : f + 1], sems.at[f]))
        copies[f].start()
    for copy in copies:
        copy.wait()


def land_kernel(
    ocean_comp,
    comp_ref,
    count_ref,
    row_ref,
    col_ref,
    weight_ref,
    got_0,
    got_1,
    got_2,
    field_hbm,
    coef_ref,
    mask_ref,
    state_hbm,
    partner_hbm,
    centre_ref,
    west_ref,
    east_ref,
    field_ref,
    state_out,
    partner_out,
    sems,
):
    fetch = pltpu.make_async_copy(field_hbm.at[:, 0:1], field_ref, sems.at[0])
    fetch.start()
    ocean = comp_ref[0] == ocean_comp
    row_count, col_count = coef_ref.shape
    part = row_ref.shape[-1] // PARTS
    slot_iota = lax.broadcasted_iota(jnp.int32, (1, part), 1)
    nt = (((1,), (1,)), ((), ()))

    def land(lists):
        for o, total_ref in ((1, centre_ref), (0, west_ref), (2, east_ref)):
            total = None
            for h, got in lists:
                count = count_ref[o, h]
                for q in range(PARTS):
                    span = slice(q * part, (q + 1) * part)
                    columns = col_ref[0, 0, o, h : h + 1, span]
                    rows = row_ref[0, 0, o, h : h + 1, span]
                    weights = weight_ref[0, 0, o, h : h + 1, span]
                    live = slot_iota + q * part < count
                    if o == 1:
                        table = wide_one_hot(columns, col_count)
                    else:
                        table = one_hot(columns - (EAST_OFFSET if o == 2 else 0), LANES)
                    masks = one_hot_masks(rows, row_count)
                    pieces = []
                    for f in range(2):
                        value = got[o, q + f * PARTS : q + f * PARTS + 1]
                        value = jnp.broadcast_to(jnp.where(live, weights * value, 0.0), (16, part))
                        pieces.append(split_halves(value))
                    left = jnp.concatenate(
                        [
                            jnp.where(mask, pieces[f][s], jnp.bfloat16(0))
                            for s in range(2)
                            for f in range(2)
                            for mask in masks
                        ],
                        axis=0,
                    )
                    product = lax.dot_general(left, table, nt, preferred_element_type=jnp.float32)
                    total = product if total is None else total + product
            size = total.shape[0] // 2
            total_ref[...] = total[:size] + total[size:]

    @pl.when(ocean)
    def _():
        land([(j, got) for j, got in enumerate((got_0, got_1, got_2))])

    @pl.when(jnp.logical_not(ocean))
    def _():
        comp = comp_ref[0]
        mine = jnp.where(comp == 0, got_0[...], jnp.where(comp == 1, got_1[...], got_2[...]))
        land([(ocean_comp, mine)])

    def far(f):
        centre = centre_ref[f * row_count : (f + 1) * row_count]
        sides = []
        for ref in (west_ref, east_ref):
            sides.append(ref[f * row_count : (f + 1) * row_count])
        return jnp.concatenate(
            [
                centre[:, :LANES] + sides[0],
                centre[:, LANES : col_count - LANES],
                centre[:, col_count - LANES :] + sides[1],
            ],
            axis=1,
        )

    first_far = far(0)
    second_far = far(1)
    partner_out[0] = first_far
    partner_out[1] = second_far
    send_partner = pltpu.make_async_copy(partner_out, partner_hbm, sems.at[1])
    send_partner.start()
    fetch.wait()
    rate = coef_ref[...] * mask_ref[...].astype(jnp.float32)
    first_own = field_ref[0, 0]
    second_own = field_ref[1, 0]
    state_out[0, 0] = first_own + rate * (first_far - first_own)
    air_second = second_own + rate * (1.2 * first_far - 0.3 * second_far - second_own)
    sea_second = second_own + rate * (1.2 * first_own - second_far)
    state_out[1, 0] = jnp.where(ocean, sea_second, air_second)
    send_state = pltpu.make_async_copy(state_out, state_hbm.at[:, 0:1], sems.at[2])
    send_state.start()
    send_partner.wait()
    send_state.wait()


def whole(array):
    return pl.BlockSpec(array.shape, functools.partial(lambda n, *i: (0,) * n, len(array.shape)))


def shards(
    state,
    courant,
    mixing,
    exchange_coef,
    sea_mask,
    margin_count,
    margin_row,
    margin_col,
    margin_weight,
):
    fields, levels, row_count, col_count = state.shape
    slots = margin_row.shape[-1]
    ocean_comp = margin_row.shape[3] - 1
    part = slots // PARTS
    tiles = lax.axis_size("tile")
    comp = lax.axis_index("comp").astype(jnp.int32).reshape(1)
    counts = margin_count.reshape(3, ocean_comp + 1)
    scalar = pl.BlockSpec(memory_space=pltpu.SMEM)
    params = pltpu.CompilerParams(vmem_limit_bytes=VMEM_LIMIT)
    packet = jax.ShapeDtypeStruct((2 * PARTS, ocean_comp * part + LANES * HALO_ROWS // 8), jnp.float32)

    to_west, to_east = pl.pallas_call(
        functools.partial(edge_kernel, ocean_comp),
        in_specs=[scalar] + [pl.BlockSpec(memory_space=pl.ANY)] * 3,
        out_specs=[pl.BlockSpec(memory_space=pltpu.VMEM)] * 2,
        out_shape=[packet] * 2,
        scratch_shapes=[
            pltpu.VMEM(margin_row.shape, jnp.int32),
            pltpu.VMEM(margin_col.shape, jnp.int32),
            pltpu.VMEM((fields, 1, row_count, LANES), jnp.float32),
            pltpu.VMEM((fields, 1, row_count, LANES), jnp.float32),
            pltpu.VMEM((fields, levels, row_count, LANES), jnp.float32),
            pltpu.VMEM((fields, levels, row_count, LANES), jnp.float32),
            pltpu.SemaphoreType.DMA((8,)),
        ],
        compiler_params=pltpu.CompilerParams(vmem_limit_bytes=FIRST_VMEM_LIMIT),
        name="edge_gather",
    )(comp, margin_row, margin_col, state)
    forward = [(i, (i + 1) % tiles) for i in range(tiles)]
    backward = [(b, a) for a, b in forward]
    from_west = lax.ppermute(to_east, "tile", forward)
    from_east = lax.ppermute(to_west, "tile", backward)

    bundle = jax.ShapeDtypeStruct((3, 2 * PARTS, part), jnp.float32)
    centre = pl.pallas_call(
        functools.partial(centre_kernel, ocean_comp),
        in_specs=[scalar] + [pl.BlockSpec(memory_space=pltpu.VMEM)] * 3,
        out_specs=pl.BlockSpec(memory_space=pltpu.VMEM),
        out_shape=bundle,
        compiler_params=params,
        name="centre_gather",
    )(comp, margin_row, margin_col, state)
    bundles = pl.pallas_call(
        functools.partial(pack_kernel, ocean_comp),
        in_specs=[scalar, scalar] + [pl.BlockSpec(memory_space=pltpu.VMEM)] * 3,
        out_specs=[pl.BlockSpec(memory_space=pltpu.VMEM)] * ocean_comp,
        out_shape=[bundle] * ocean_comp,
        compiler_params=params,
        name="pack",
    )(comp, counts, centre, from_west, from_east)
    got = []
    for g in range(ocean_comp):
        swap = [(i, i ^ (g ^ ocean_comp)) for i in range(ocean_comp + 1)]
        got.append(lax.ppermute(bundles[g], "comp", swap))

    moved = pl.pallas_call(
        functools.partial(transport_kernel, ocean_comp * part),
        in_specs=[pl.BlockSpec(memory_space=pltpu.VMEM)] * 5 + [pl.BlockSpec(memory_space=pl.ANY)],
        out_specs=pl.BlockSpec(memory_space=pl.ANY),
        out_shape=jax.ShapeDtypeStruct(state.shape, jnp.float32),
        scratch_shapes=[pltpu.VMEM(state.shape, jnp.float32), pltpu.SemaphoreType.DMA((fields,))],
        compiler_params=params,
        name="transport",
    )(state, courant, mixing, from_west, from_east, bundles[0])

    level = (fields, 1, row_count, col_count)
    partner = jax.ShapeDtypeStruct((fields, row_count, col_count), jnp.float32)
    local = pl.BlockSpec(memory_space=pltpu.VMEM)
    anywhere = pl.BlockSpec(memory_space=pl.ANY)
    return pl.pallas_call(
        functools.partial(land_kernel, ocean_comp),
        in_specs=[scalar, scalar] + [local] * 6 + [anywhere, local, local],
        out_specs=[anywhere, anywhere],
        out_shape=[jax.ShapeDtypeStruct(state.shape, jnp.float32), partner],
        scratch_shapes=[
            pltpu.VMEM((2 * row_count, col_count), jnp.float32),
            pltpu.VMEM((2 * row_count, LANES), jnp.float32),
            pltpu.VMEM((2 * row_count, LANES), jnp.float32),
            pltpu.VMEM(level, jnp.float32),
            pltpu.VMEM(level, jnp.float32),
            pltpu.VMEM(partner.shape, jnp.float32),
            pltpu.SemaphoreType.DMA((3,)),
        ],
        input_output_aliases={8: 0},
        compiler_params=params,
        name="land",
    )(
        comp,
        counts,
        margin_row,
        margin_col,
        margin_weight,
        *got,
        moved,
        exchange_coef,
        sea_mask,
    )


def solution(mesh):
    in_specs = (
        P(None, None, "comp", "tile"),
        P(None, "comp"),
        P(None, "comp"),
        P("comp", "tile"),
        P("comp", "tile"),
        P("comp", "tile", None, None),
        P("comp", "tile", None, None, None),
        P("comp", "tile", None, None, None),
        P("comp", "tile", None, None, None),
    )
    out_specs = (P(None, None, "comp", "tile"), P(None, "comp", "tile"))
    return jax.shard_map(shards, mesh=mesh, in_specs=in_specs, out_specs=out_specs, check_vma=False)
```
